32 devices in a mesh: row: 2 (over y), col: 16 (over z, x, core).
Axes of the slice: x: 2, y: 2, z: 4, core: 2. Of those that a mesh axis runs over, the one named last changes fastest.
Arguments:
- ancestor_inv: float32 [16384, 16384], P('row', 'col'), may hold values from -0.0625 to 0.0625
- factor_rows: float32 [16384, 768], P(('row', 'col')), may hold values from -1.2 to 1.2
- diagonal_inv: float32 [3, 256, 256], replicated, may hold values from -6 to 6
- fill_list: int32 [3, 64], replicated, may hold values 0 or 1
Outputs:
- column_block: float32 [16384, 768], P(('row', 'col'))
- diagonal_block: float32 [3, 256, 256], replicated
The draws below stay inside these ranges and needn't reach their ends.
All inputs are finite; a program needn't handle non-finite values.
Results may differ from the reference program's by a relative error of at most 0.000071.
Values sent between devices are 32-bit elements; how exact they have to be, the bound alone decides.
No kernel may reach another device: no remote copies, remote signals or barrier semaphores. Data moves between devices by JAX's collectives and lax.ppermute only.
A program may use at most 128 MiB of HBM per device.

```python
import jax
import jax.numpy as jnp
from jax import lax

R = 16384
W = 256
SIBS = 3
TILE = 256
NB = 64


def touch_ends(result, stream_key, low, top_value):
    shape = result.shape
    index_at = [jax.random.randint(jax.random.fold_in(stream_key, axis), (), 0, shape[axis]) for axis in range(len(shape))]
    result = result.at[tuple(index_at)].set(low)
    longest = shape.index(max(shape))
    index_at[longest] = (index_at[longest] + 1) % shape[longest]
    return result.at[tuple(index_at)].set(top_value)


def raised(array, rng, source, target, blocks, factor):
    owner, partner = [(jnp.arange(array.shape[dim]) // (array.shape[dim] // blocks)).reshape([-1 if axis == dim else 1 for axis in range(array.ndim)]) for dim in (source, target)]
    chosen = jax.random.permutation(rng, blocks)[partner]
    strong = (owner == chosen) | (owner == (partner + blocks // 2) % blocks)
    return jnp.where(strong, factor * array, array)


def block_scale(own_key, dims, cuts, least, high):
    def one(position, blocks):
        steps = jax.random.uniform(jax.random.fold_in(jax.random.fold_in(own_key, 6), position), (blocks,), jnp.float32, least / len(cuts), high / len(cuts))
        return jnp.repeat(jnp.exp(steps), dims[position] // blocks).reshape((-1,) + (1,) * (len(dims) - position - 1))

    gain = one(*cuts[0])
    for cut in cuts[1:]:
        gain = gain * one(*cut)
    return gain


def normal_values(stream_key, shape, scale, bound, pieces=(), kind=jnp.bfloat16):
    array = jax.random.normal(stream_key, shape, jnp.float32) * scale
    if len(pieces) > 0:
        array = block_scale(stream_key, shape, pieces, -0.22, 0.18) * array
    return jnp.clip(array, min=-bound, max=bound).astype(kind)


def bell_draw_with(rng, dims, width, most, cuts, heavy, held_as=jnp.bfloat16):
    drawn = width * jax.random.normal(rng, dims, jnp.float32)
    if cuts:
        drawn = drawn * block_scale(rng, dims, cuts, -0.22, 0.18)
    return jnp.clip(raised(drawn, jax.random.fold_in(rng, 3), *heavy), -most, most).astype(held_as)


def setup_inputs(seed: int = 0) -> dict:
    seeds = jax.random.split(jax.random.key(seed), 5)
    ancestor_inv = bell_draw_with(seeds[0], (R, R), R ** -0.5, 0.0625, ((0, 2), (1, 16)), (1, 0, 16, 2.0), jnp.float32)
    factor_rows = normal_values(seeds[1], (R, SIBS * W), 0.2, 1.2, ((0, 32),), jnp.float32)
    diagonal_inv = normal_values(seeds[2], (SIBS, W, W), 1.0, 6.0, (), jnp.float32)
    fill_list = touch_ends((jax.random.randint(seeds[3], (SIBS, NB), 0, 2) < 1).astype(jnp.int32), jax.random.fold_in(seeds[3], 1), 0, 1)
    return {"ancestor_inv": ancestor_inv, "factor_rows": factor_rows, "diagonal_inv": diagonal_inv, "fill_list": fill_list}


def reference(ancestor_inv, factor_rows, diagonal_inv, fill_list):
    tile_index = jnp.arange(R, dtype=jnp.int32) // TILE
    one_hot = (tile_index[:, None] == jnp.arange(NB, dtype=jnp.int32)[None, :]).astype(jnp.float32)
    row_mask = jnp.dot(one_hot, fill_list.T.astype(jnp.float32), precision=lax.Precision.HIGHEST)
    wide_mask = jnp.repeat(row_mask, W, axis=1)
    masked = factor_rows * wide_mask
    product = jnp.dot(ancestor_inv, masked, precision=lax.Precision.HIGHEST)
    column_block = -product * wide_mask
    left_side = masked.reshape(R, SIBS, W)
    right_side = column_block.reshape(R, SIBS, W)
    update = jnp.einsum("rkw,rkv->kwv", left_side, right_side, precision=lax.Precision.HIGHEST)
    return column_block, diagonal_inv - update
```

```python
import functools

import jax
import jax.numpy as jnp
import numpy as np
from jax import lax
from jax.experimental import pallas as pl
from jax.experimental.pallas import tpu as pltpu
from jax.sharding import PartitionSpec as P

W = 256
SIBS = 3
TILE = 256
LANES = 128
CHUNKS = W // LANES
VMEM_LIMIT = 32 * 1024 * 1024
MULTIPLY_VMEM = 24 * 1024 * 1024
STRIPS = (((0, 2, 0), (2, 4, 1)), ((0, 2, 0), (2, 4, 1)))
SLOTS = 6
LONG = pl.CostEstimate(flops=10**11, bytes_accessed=1, transcendentals=0)
TOKEN = jax.ShapeDtypeStruct((1,), jnp.int32)
SMEM = pltpu.SMEM
VMEM = pltpu.VMEM


class Plan:
    def __init__(self, row_devices, col_devices, own_rows, band_rows, block_rows):
        self.row_devices, self.col_devices = row_devices, col_devices
        self.own_rows, self.band_rows, self.block_rows = own_rows, band_rows, block_rows
        self.bits = col_devices.bit_length() - 1
        self.high = min(TILE, own_rows)
        self.half = self.high // 2
        self.sub = TILE // self.high
        self.per = own_rows // self.high
        self.tile_rows = band_rows // self.high
        self.blocks = band_rows // TILE
        self.tiles = self.tile_rows * SIBS
        first = list(range(1, self.bits))
        second = [2, 1] + first[2:] if self.bits > 2 else first
        self.steps = len(first)
        self.orders = (first, second)
        unit = self.half // 4
        self.strips = [[(a * unit, b * unit, order) for a, b, order in chunk] for chunk in STRIPS]

    def sequence(self, order, step):
        same = self.orders[0] == self.orders[1] or step > 1
        return (0 if same else order) * self.steps + step

    def pos_row(self, order, step):
        return 3 * self.sequence(order, step)

    def give_row(self, order, step):
        return 1 + self.pos_row(order, step)

    def hold_row(self, order, step):
        return 2 + self.pos_row(order, step)

    def block_row(self, k):
        return 6 * self.steps + k

    @property
    def count_row(self):
        return 6 * self.steps + SIBS

    def give_count(self, order, step):
        return 2 * self.sequence(order, step)

    def hold_count(self, order, step):
        return 1 + self.give_count(order, step)

    def block_count(self, k):
        return 4 * self.steps + k


def plan_kernel(plan, where_ref, fill_ref, table_ref):
    row_index, col_index = where_ref[0], where_ref[1]
    every = [(order, step) for order in range(2) for step in range(plan.steps)]
    sequences = list({plan.sequence(*each): each for each in every}.values())
    zero = jnp.int32(0)

    def one_block(block, counts):
        result = []
        for k in range(SIBS):
            table_ref[plan.block_row(k), counts[k]] = block
            result.append(counts[k] + fill_ref[k, row_index * plan.blocks + block])
        return tuple(result)

    counts = lax.fori_loop(0, plan.blocks, one_block, (zero,) * SIBS)
    for k in range(SIBS):
        table_ref[plan.count_row, plan.block_count(k)] = counts[k]

    def one_tile(tile, counts):
        tile_row, sibling = tile // SIBS, tile % SIBS
        apart = (tile_row // plan.per) ^ col_index

        def place(counts):
            result = []
            for number, (order, step) in enumerate(sequences):
                held, sent = counts[2 * number], counts[2 * number + 1]
                bits = plan.orders[order]
                earlier = sum(1 << bit for bit in bits[:step])
                here = 1 << bits[step]
                table_ref[plan.pos_row(order, step), tile] = held
                table_ref[plan.hold_row(order, step), held] = tile
                table_ref[plan.give_row(order, step), sent] = tile
                keeps = (apart & (earlier | here)) == 0
                gives = (apart & (earlier | here)) == here
                result += [held + keeps.astype(jnp.int32), sent + gives.astype(jnp.int32)]
            return tuple(result)

        active = fill_ref[sibling, (row_index * plan.tile_rows + tile_row) // plan.sub] != 0
        return lax.cond(active, place, lambda counts: counts, counts)

    counts = lax.fori_loop(0, plan.tiles, one_tile, (zero,) * (2 * len(sequences)))
    for number, (order, step) in enumerate(sequences):
        table_ref[plan.count_row, plan.hold_count(order, step)] = counts[2 * number]
        table_ref[plan.count_row, plan.give_count(order, step)] = counts[2 * number + 1]


def make_plan(plan, where, fill_list):
    width = -(-(plan.tiles + 1) // 128) * 128
    return pl.pallas_call(
        functools.partial(plan_kernel, plan),
        out_shape=jax.ShapeDtypeStruct((plan.count_row + 1, width), jnp.int32),
        in_specs=[pl.BlockSpec(memory_space=SMEM)] * 2,
        out_specs=pl.BlockSpec(memory_space=SMEM),
        name="plan",
    )(where, fill_list)


def split_high_low(values):
    high = values.astype(jnp.bfloat16)
    return high, (values - high.astype(jnp.float32)).astype(jnp.bfloat16)


def multiply_kernel(plan, k, column, where_ref, fill_ref, table_ref, token_ref, inverse_ref, *refs):
    pieces = refs[: plan.row_devices]
    keep_ref, send_ref, done_ref, factor_ref, rows_ref, high_ref, low_ref, total_ref, sems = refs[plan.row_devices :]
    done_ref[0] = token_ref[0]
    row_index, col_index = where_ref[0], where_ref[1]
    core = col_index % 2
    count = table_ref[plan.count_row, plan.block_count(k)]

    def fetch(number, slot):
        start = pl.multiple_of(table_ref[plan.block_row(k), number] * TILE, TILE)
        return pltpu.make_async_copy(inverse_ref.at[pl.ds(start, TILE), :], rows_ref.at[slot], sems.at[slot])

    for ahead in range(SLOTS - 1):

        @pl.when(ahead < count)
        def _(ahead=ahead):
            fetch(ahead, ahead).start()

    for shift in range(plan.row_devices):
        source = lax.rem(row_index - shift + plan.row_devices, plan.row_devices)
        for part in range(plan.per):
            start = pl.multiple_of(source * plan.own_rows + part * plan.high, plan.high)
            filled = fill_ref[k, (col_index * plan.block_rows + start) // TILE].astype(jnp.float32)
            piece = pieces[shift][part * plan.high : (part + 1) * plan.high, column : column + LANES]
            high, low = split_high_low(piece * filled)
            factor_ref[pl.ds(start, plan.high), :LANES] = high
            factor_ref[pl.ds(start, plan.high), LANES:] = low

    def one(number, carry):
        slot = lax.rem(number, SLOTS)
        fetch(number, slot).wait()

        @pl.when(number + SLOTS - 1 < count)
        def _():
            fetch(number + SLOTS - 1, lax.rem(number + SLOTS - 1, SLOTS)).start()

        high, low = split_high_low(rows_ref[slot])
        high_ref[...] = high
        low_ref[...] = low
        wide = jnp.dot(high_ref[...], factor_ref[...], preferred_element_type=jnp.float32)
        narrow = jnp.dot(low_ref[...], factor_ref[:, :LANES], preferred_element_type=jnp.float32)
        total_ref[...] = wide[:, :LANES] + (wide[:, LANES:] + narrow)
        first = table_ref[plan.block_row(k), number] * plan.sub
        for part in range(plan.sub):
            near = pl.multiple_of(part * plan.high + core * plan.half, plan.half)
            far = pl.multiple_of(part * plan.high + (1 - core) * plan.half, plan.half)
            keep_ref[first + part] = total_ref[pl.ds(near, plan.half), :]
            send_ref[first + part] = total_ref[pl.ds(far, plan.half), :]
        return carry

    lax.fori_loop(0, count, one, 0)


def multiply(plan, k, column, where, fill_list, table, token, inverse, pieces):
    shape = jax.ShapeDtypeStruct((plan.tile_rows, plan.half, LANES), jnp.float32)
    smem, vmem = pl.BlockSpec(memory_space=SMEM), pl.BlockSpec(memory_space=VMEM)
    return pl.pallas_call(
        functools.partial(multiply_kernel, plan, k, column),
        out_shape=(shape, shape, TOKEN),
        in_specs=[smem, smem, smem, smem, pl.BlockSpec(memory_space=pl.ANY)] + [vmem] * len(pieces),
        out_specs=(vmem, vmem, smem),
        scratch_shapes=[
            VMEM((plan.block_rows, 2 * LANES), jnp.bfloat16),
            VMEM((SLOTS, TILE, plan.block_rows), jnp.float32),
            VMEM((TILE, plan.block_rows), jnp.bfloat16),
            VMEM((TILE, plan.block_rows), jnp.bfloat16),
            VMEM((TILE, LANES), jnp.float32),
            pltpu.SemaphoreType.DMA((SLOTS,)),
        ],
        compiler_params=pltpu.CompilerParams(vmem_limit_bytes=MULTIPLY_VMEM),
        cost_estimate=LONG,
        name="multiply",
    )(where, fill_list, table, token, inverse, *pieces)


def call_local(kernel, out_shape, tables, token, operands, name, scratch=(), ahead=()):
    vmem, smem = pl.BlockSpec(memory_space=VMEM), pl.BlockSpec(memory_space=SMEM)

    def body(*refs):
        tables_in, token_ref, rest = refs[: len(tables)], refs[len(tables)], refs[len(tables) + len(ahead) + 1 :]
        last = len(operands) + len(out_shape)
        rest[last][0] = token_ref[0]
        kernel(*tables_in, *rest[:last], *rest[last + 1 :])

    return pl.pallas_call(
        body,
        out_shape=tuple(out_shape) + (TOKEN,),
        in_specs=[smem] * (len(tables) + 1) + [pl.BlockSpec(memory_space=pl.ANY)] * len(ahead) + [vmem] * len(operands),
        out_specs=(vmem,) * len(out_shape) + (smem,),
        scratch_shapes=scratch,
        compiler_params=pltpu.CompilerParams(vmem_limit_bytes=VMEM_LIMIT),
        cost_estimate=LONG,
        name=name,
    )(*tables, token, *ahead, *operands)


def tile_lists(plan, table_ref, step, order, outs):
    yield outs[0], plan.give_row(order, step), table_ref[plan.count_row, plan.give_count(order, step)]
    yield outs[1], plan.hold_row(order, step), table_ref[plan.count_row, plan.hold_count(order, step)]


def relay_kernel(in_ref, out_ref):
    out_ref[...] = in_ref[...]


def later_kernel(in_ref, out_ref):
    for k in range(SIBS):
        start = k * W + LANES
        out_ref[:, k * LANES : (k + 1) * LANES] = in_ref[:, start : start + LANES]


def merge_kernel(plan, strips, table_ref, *refs):
    keep, core, outs = refs[:SIBS], refs[SIBS : 2 * SIBS], refs[2 * SIBS :]
    for number, (first, last, order) in enumerate(strips):
        for out_ref, row, count in tile_lists(plan, table_ref, 0, order, outs[2 * number : 2 * number + 2]):

            def one(slot, carry, out_ref=out_ref, row=row, first=first, last=last):
                tile = table_ref[row, slot]
                tile_row, sibling = tile // SIBS, tile % SIBS
                for k in range(SIBS):

                    @pl.when(sibling == k)
                    def _(k=k):
                        out_ref[slot] = keep[k][tile_row, first:last, :] + core[k][tile_row, first:last, :]

                return carry

            lax.fori_loop(0, count, one, 0)


def step_kernel(plan, strips, step, table_ref, *refs):
    size = len(strips)
    for number, (_, _, order) in enumerate(strips):
        held_ref, came_ref = refs[number], refs[size + number]
        outs = refs[2 * size + 2 * number : 2 * size + 2 * number + 2]
        for out_ref, row, count in tile_lists(plan, table_ref, step, order, outs):

            def one(slot, carry, out_ref=out_ref, row=row, order=order, held_ref=held_ref, came_ref=came_ref):
                place = table_ref[plan.pos_row(order, step - 1), table_ref[row, slot]]
                out_ref[slot] = held_ref[place] + came_ref[place]
                return carry

            lax.fori_loop(0, count, one, 0)


def strip_shapes(cap, strip):
    return (jax.ShapeDtypeStruct((cap, strip[1] - strip[0], LANES), jnp.float32),) * 2


def collect_kernel(plan, strips, where_ref, fill_ref, table_ref, *refs):
    size = len(strips)
    held, came, (near_ref, far_ref) = refs[:size], refs[size : 2 * size], refs[2 * size :]
    row_index, col_index = where_ref[0], where_ref[1]
    for out_ref, owner in ((near_ref, col_index), (far_ref, col_index ^ 1)):
        for part in range(plan.per):
            for k in range(SIBS):
                tile_row = owner * plan.per + part
                tile = tile_row * SIBS + k
                active = fill_ref[k, (row_index * plan.tile_rows + tile_row) // plan.sub] != 0
                place = part * SIBS + k

                @pl.when(active)
                def _(out_ref=out_ref, tile=tile, place=place):
                    for number, (first, last, order) in enumerate(strips):
                        source = table_ref[plan.pos_row(order, plan.steps - 1), tile]
                        out_ref[place, first:last, :] = -(held[number][source] + came[number][source])

                @pl.when(jnp.logical_not(active))
                def _(out_ref=out_ref, place=place):
                    out_ref[place] = jnp.zeros(out_ref.shape[1:], jnp.float32)


def finish_kernel(plan, where_ref, factor_ref, *refs):
    parts, (block_ref, term_ref) = refs[: 2 * CHUNKS], refs[2 * CHUNKS :]
    core = where_ref[1] % 2
    for chunk in range(CHUNKS):
        near_ref, far_ref = parts[2 * chunk], parts[2 * chunk + 1]
        for part in range(plan.per):
            near = pl.multiple_of(part * plan.high + core * plan.half, plan.half)
            far = pl.multiple_of(part * plan.high + (1 - core) * plan.half, plan.half)
            for k in range(SIBS):
                columns = slice(k * W + chunk * LANES, k * W + (chunk + 1) * LANES)
                block_ref[pl.ds(near, plan.half), columns] = near_ref[part * SIBS + k]
                block_ref[pl.ds(far, plan.half), columns] = far_ref[part * SIBS + k]
    for k in range(SIBS):
        columns = slice(k * W, (k + 1) * W)
        term_ref[columns, :] = lax.dot_general(
            factor_ref[:, columns],
            block_ref[:, columns],
            (((0,), (0,)), ((), ())),
            precision=lax.Precision.HIGHEST,
            preferred_element_type=jnp.float32,
        )


def toggled(value, mask, devices):
    return lax.ppermute(value, ("row", "col"), [(i, i ^ mask) for i in range(devices)])


def sum_everywhere(plan, value):
    cols, devices = plan.col_devices, plan.row_devices * plan.col_devices
    me = lax.axis_index("row") * cols + lax.axis_index("col")
    masks = [1 << bit for bit in range(devices.bit_length() - 1)]
    row_masks = [m for m in masks if m >= cols]
    col_masks = [m for m in masks if m < cols]
    rest = col_masks[2:] + row_masks[1:]
    groups = [col_masks[:1], col_masks[1:2] + row_masks[:1]]
    groups += [rest[i : i + 2] for i in range(0, len(rest), 2)]

    def member(group):
        return sum(((me & mask) != 0).astype(jnp.int32) << n for n, mask in enumerate(group))

    def spread(group, number):
        return sum(mask for n, mask in enumerate(group) if number >> n & 1)

    for group in groups[:-1]:
        size = 1 << len(group)
        rows = value.shape[0] // size
        mine = member(group)
        sent = [
            toggled(lax.dynamic_slice_in_dim(value, (mine ^ d) * rows, rows, 0), spread(group, d), devices)
            for d in range(1, size)
        ]
        own = lax.dynamic_slice_in_dim(value, mine * rows, rows, 0)
        value = functools.reduce(jnp.add, sent, own)
    group = groups[-1]
    arrived = [toggled(value, spread(group, d), devices) for d in range(1, 1 << len(group))]
    mine = member(group)
    whole = jnp.stack([value] + arrived)
    ordered = [lax.dynamic_index_in_dim(whole, mine ^ n, 0, False) for n in range(1 << len(group))]
    value = functools.reduce(jnp.add, ordered)
    for group in reversed(groups[:-1]):
        size = 1 << len(group)
        mine = member(group)
        parts = [value] + [toggled(value, spread(group, d), devices) for d in range(1, size)]
        whole = jnp.stack(parts)
        value = jnp.concatenate([lax.dynamic_index_in_dim(whole, mine ^ n, 0, False) for n in range(size)])
    return value


def cross(plan, value):
    rows, cols = plan.row_devices, plan.col_devices
    if rows != 2:
        return value
    pairs = [(r * cols + c, (c & 1) * cols + (c & ~1 | r)) for r in range(rows) for c in range(cols)]
    return lax.ppermute(value, ("row", "col"), pairs)


def home(plan, value):
    rows, cols = plan.row_devices, plan.col_devices
    if rows != 2:
        pairs = [(rows * j + h, h * cols + j) for j in range(cols) for h in range(rows)]
    else:
        pairs = []
        for y in range(rows):
            for c in range(cols):
                pairs.append((y * cols + c, y * cols + ((c & 1) * cols + (c & ~1 | y)) // 2))
    return lax.ppermute(value, ("row", "col"), pairs)


def sparse(plan, caps, ancestor_inv, factor_rows, diagonal_inv, fill_list):
    rows, cols = plan.row_devices, plan.col_devices
    where = jnp.stack([lax.axis_index("row"), lax.axis_index("col")]).astype(jnp.int32)
    table = make_plan(plan, where, fill_list)
    pair = [(i, i ^ 1) for i in range(cols)]
    token = jnp.zeros(TOKEN.shape, TOKEN.dtype)
    tile_set = jax.ShapeDtypeStruct((plan.per * SIBS, plan.half, LANES), jnp.float32)

    def over_rows(own):
        turns = [[(i, (i + shift) % rows) for i in range(rows)] for shift in range(1, rows)]
        return [own] + [lax.ppermute(own, "row", turn) for turn in turns]

    def product(k, column, pieces, token):
        near, far, token = multiply(plan, k, column, where, fill_list, table, token, ancestor_inv, pieces)
        return [near, lax.ppermute(far, "col", pair)], token

    def relay(value, token):
        shape = jax.ShapeDtypeStruct(value.shape, value.dtype)
        return call_local(relay_kernel, (shape,), [], token, [value], "relay")

    def later_columns(token):
        shape = jax.ShapeDtypeStruct((factor_rows.shape[0], SIBS * LANES), jnp.float32)
        return call_local(later_kernel, (shape,), [], token, [factor_rows], "later_columns")

    def exchange(chunk, step, made):
        strips = plan.strips[chunk]
        held, came = [], []
        for number, strip in enumerate(strips):
            bit = 1 << plan.orders[strip[2]][step]
            came.append(lax.ppermute(made[2 * number], "col", [(i, i ^ bit) for i in range(cols)]))
            held.append(made[2 * number + 1])
        return held + came

    def merge(chunk, operands, token):
        strips = plan.strips[chunk]
        shapes = sum((strip_shapes(caps[1], strip) for strip in strips), ())
        *made, token = call_local(functools.partial(merge_kernel, plan, strips), shapes, [table], token, operands, "merge")
        return exchange(chunk, 0, made), token

    def step(chunk, number, operands, token):
        strips = plan.strips[chunk]
        shapes = sum((strip_shapes(caps[number + 1], strip) for strip in strips), ())
        kernel = functools.partial(step_kernel, plan, strips, number)
        *made, token = call_local(kernel, shapes, [table], token, operands, "step")
        return exchange(chunk, number, made), token

    def collect(chunk, operands, token):
        kernel = functools.partial(collect_kernel, plan, plan.strips[chunk])
        tables = [where, fill_list, table]
        near, far, token = call_local(kernel, (tile_set, tile_set), tables, token, operands, "collect")
        return [near, lax.ppermute(far, "col", pair)], token

    def finish(parts, token):
        shapes = (
            jax.ShapeDtypeStruct(factor_rows.shape, jnp.float32),
            jax.ShapeDtypeStruct((SIBS * W, W), jnp.float32),
        )
        kernel = functools.partial(finish_kernel, plan)
        return call_local(kernel, shapes, [where], token, [factor_rows] + parts, "finish")

    def sums(made):
        return [near for near, _ in made] + [core for _, core in made]

    pieces = []
    for k in range(SIBS):
        columns = factor_rows[:, k * W : k * W + LANES]
        pieces.append(over_rows(home(plan, cross(plan, columns))))
    made = [None] * SIBS
    made[0], token = product(0, 0, pieces[0], token)
    columns, token = later_columns(token)
    made[1], token = product(1, 0, pieces[1], token)
    columns, token = relay(cross(plan, columns), token)
    made[2], token = product(2, 0, pieces[2], token)
    first, token = merge(0, sums(made), token)
    columns, token = relay(home(plan, columns), token)
    later = over_rows(columns)
    first, token = step(0, 1, first, token)
    made[0], token = product(0, 0, later, token)
    made[1], token = product(1, LANES, later, token)
    first, token = step(0, 2, first, token)
    made[2], token = product(2, 2 * LANES, later, token)
    second, token = merge(1, sums(made), token)
    for number in range(3, plan.steps):
        first, token = step(0, number, first, token)
        second, token = step(1, number - 2, second, token)
    first, token = collect(0, first, token)
    second, token = step(1, plan.steps - 2, second, token)
    second, token = step(1, plan.steps - 1, second, token)
    second, token = collect(1, second, token)
    column_block, term, token = finish(first + second, token)
    update = sum_everywhere(plan, term).reshape(diagonal_inv.shape)
    return column_block, diagonal_inv - update


def row_masks(fill_list, first_row, row_count):
    positions = first_row + jnp.arange(row_count, dtype=jnp.int32)
    tile_index = positions // TILE
    one_hot = (
        tile_index[:, None] == jnp.arange(fill_list.shape[1], dtype=jnp.int32)[None, :]
    ).astype(jnp.float32)
    return jnp.dot(one_hot, fill_list.T.astype(jnp.float32), precision=lax.Precision.HIGHEST)


def dense(ancestor_inv, factor_rows, diagonal_inv, fill_list):
    row_devices, col_devices = lax.axis_size("row"), lax.axis_size("col")
    group_span = col_devices // row_devices
    own_rows = factor_rows.shape[0]
    band_rows, block_rows = ancestor_inv.shape
    row_index, col_index = lax.axis_index("row"), lax.axis_index("col")
    first_row = row_index * band_rows + col_index * own_rows
    wide_mask = jnp.repeat(row_masks(fill_list, first_row, own_rows), W, axis=1)
    masked = factor_rows * wide_mask
    band = lax.all_gather(masked, "col", axis=0, tiled=True)
    section = lax.dynamic_slice_in_dim(band, col_index % group_span * block_rows, block_rows, 0)
    section = jnp.where(row_index == col_index // group_span, section, jnp.zeros_like(section))
    product = jnp.dot(ancestor_inv, lax.psum(section, "row"), precision=lax.Precision.HIGHEST)
    summed = lax.psum_scatter(product, "col", scatter_dimension=0, tiled=True)
    column_block = -summed * wide_mask
    left_side = masked.reshape(own_rows, SIBS, W)
    right_side = column_block.reshape(own_rows, SIBS, W)
    local_term = jnp.einsum("rkw,rkv->kwv", left_side, right_side, precision=lax.Precision.HIGHEST)
    update = lax.psum(local_term, ("row", "col"))
    return column_block, diagonal_inv - update


def fill_groups(plan):
    devices = np.arange(plan.row_devices * plan.col_devices)
    columns, levels = [], []
    for order in plan.orders:
        for step in range(plan.steps + 1):
            mask = sum(1 << bit for bit in order[:step])
            key = (devices // plan.col_devices) * plan.col_devices + (devices % plan.col_devices & mask)
            for value in np.unique(key):
                columns.append(key == value)
                levels.append(step)
    member = np.stack(columns, axis=1).astype(np.float32)
    return np.repeat(member, plan.per, axis=0), np.array(levels)


SHARES = (((96, 96), (30, 48), (17, 24), (10, 12), (6, 6)), ((96, 96), (37, 48), (21, 24), (12, 12), (6, 6)))


def local(ancestor_inv, factor_rows, diagonal_inv, fill_list):
    plan = Plan(
        lax.axis_size("row"), lax.axis_size("col"), factor_rows.shape[0], ancestor_inv.shape[0], ancestor_inv.shape[1]
    )
    member, levels = fill_groups(plan)
    block_of = np.arange(member.shape[0]) // plan.sub
    spread = np.zeros((fill_list.shape[1], member.shape[1]), np.float32)
    np.add.at(spread, block_of, member)
    per_block = jnp.sum(fill_list, axis=0).astype(jnp.float32)
    found = jnp.sum(per_block[:, None] * spread, axis=0)
    limits, branches = [], []
    for shares in SHARES:
        caps = []
        for level in range(plan.steps + 1):
            size = plan.tiles >> level
            part, full = shares[min(level, len(shares) - 1)]
            caps.append(min(size, -(-size * part // full)))
        limits.append([caps[level] for level in levels])
        branches.append(functools.partial(sparse, plan, caps))
    branches.append(dense)
    index = jnp.sum(jnp.any(found[None, :] > np.array(limits, np.float32), axis=1).astype(jnp.int32))
    return lax.switch(index, branches, ancestor_inv, factor_rows, diagonal_inv, fill_list)


def solution(mesh):
    placed = (P("row", "col"), P(("row", "col"), None), P(), P())
    return jax.shard_map(
        local, mesh=mesh, in_specs=placed, out_specs=(P(("row", "col"), None), P()), check_vma=False
    )
```

```python
import functools

import jax
import jax.numpy as jnp
import numpy as np
from jax import lax
from jax.experimental import pallas as pl
from jax.experimental.pallas import tpu as pltpu
from jax.sharding import PartitionSpec as P

W = 256
SIBS = 3
TILE = 256
VMEM_LIMIT = 32 * 1024 * 1024
MULTIPLY_VMEM = 32 * 1024 * 1024
STRIPS = (((0, 2, 0), (2, 4, 1)), ((0, 2, 0), (2, 4, 1)), ((0, 2, 0), (2, 4, 1)))
SLOTS = 6
TOKEN = jax.ShapeDtypeStruct((1,), jnp.int32)
LONG = pl.CostEstimate(flops=10**11, bytes_accessed=1, transcendentals=0)
SMEM = pltpu.SMEM
VMEM = pltpu.VMEM


class Plan:
    def __init__(self, row_devices, col_devices, own_rows, band_rows, block_rows):
        self.row_devices, self.col_devices = row_devices, col_devices
        self.own_rows, self.band_rows, self.block_rows = own_rows, band_rows, block_rows
        self.bits = col_devices.bit_length() - 1
        self.high = min(TILE, own_rows)
        self.half = self.high // 2
        self.sub = TILE // self.high
        self.per = own_rows // self.high
        self.tile_rows = band_rows // self.high
        self.blocks = band_rows // TILE
        first = list(range(1, self.bits))
        second = [2, 1] + first[2:] if self.bits > 2 else first
        self.steps = len(first)
        self.orders = (first, second)
        unit = self.half // 4
        self.strips = [[(a * unit, b * unit, order) for a, b, order in sibling] for sibling in STRIPS]
        every = [(order, step) for order in range(2) for step in range(self.steps)]
        self.sequences = list({self.sequence(*each): each for each in every}.values())

    @property
    def table_rows(self):
        return 3 + 6 * self.steps

    def block_row(self, k):
        return k * self.table_rows

    def rank_row(self, k):
        return k * self.table_rows + 1

    def count_row(self, k):
        return k * self.table_rows + 2

    def sequence(self, order, step):
        same = self.orders[0] == self.orders[1] or step > 1
        return (0 if same else order) * self.steps + step

    def pos_row(self, k, order, step):
        return k * self.table_rows + 3 + 3 * self.sequence(order, step)

    def give_row(self, k, order, step):
        return 1 + self.pos_row(k, order, step)

    def hold_row(self, k, order, step):
        return 2 + self.pos_row(k, order, step)

    def give_count(self, order, step):
        return 1 + 2 * self.sequence(order, step)

    def hold_count(self, order, step):
        return 1 + self.give_count(order, step)


def plan_kernel(plan, where_ref, fill_ref, table_ref):
    row_index, col_index = where_ref[0], where_ref[1]
    sequences = plan.sequences
    zero = jnp.int32(0)

    def one_sibling(k, carry):
        def one_block(block, count):
            table_ref[plan.block_row(k), count] = block
            table_ref[plan.rank_row(k), block] = count
            return count + fill_ref[k, row_index * plan.blocks + block]

        table_ref[plan.count_row(k), 0] = lax.fori_loop(0, plan.blocks, one_block, zero)

        def one_tile(tile, counts):
            apart = (tile // plan.per) ^ col_index

            def place(counts):
                result = []
                for number, (order, step) in enumerate(sequences):
                    held, sent = counts[2 * number], counts[2 * number + 1]
                    bits = plan.orders[order]
                    earlier = sum(1 << bit for bit in bits[:step])
                    here = 1 << bits[step]
                    table_ref[plan.pos_row(k, order, step), tile] = held
                    table_ref[plan.hold_row(k, order, step), held] = tile
                    table_ref[plan.give_row(k, order, step), sent] = tile
                    keeps = (apart & (earlier | here)) == 0
                    gives = (apart & (earlier | here)) == here
                    result += [held + keeps.astype(jnp.int32), sent + gives.astype(jnp.int32)]
                return tuple(result)

            active = fill_ref[k, (row_index * plan.tile_rows + tile) // plan.sub] != 0
            return lax.cond(active, place, lambda counts: counts, counts)

        counts = lax.fori_loop(0, plan.tile_rows, one_tile, (zero,) * (2 * len(sequences)))
        for number, (order, step) in enumerate(sequences):
            table_ref[plan.count_row(k), plan.hold_count(order, step)] = counts[2 * number]
            table_ref[plan.count_row(k), plan.give_count(order, step)] = counts[2 * number + 1]
        return carry

    lax.fori_loop(0, SIBS, one_sibling, zero)


def make_plan(plan, where, fill_list):
    width = -(-max(plan.tile_rows + 1, 3 + 4 * plan.steps) // 128) * 128
    return pl.pallas_call(
        functools.partial(plan_kernel, plan),
        out_shape=jax.ShapeDtypeStruct((SIBS * plan.table_rows, width), jnp.int32),
        in_specs=[pl.BlockSpec(memory_space=SMEM)] * 2,
        out_specs=pl.BlockSpec(memory_space=SMEM),
        name="plan",
    )(where, fill_list)


def split_high_low(values):
    high = values.astype(jnp.bfloat16)
    return high, (values - high.astype(jnp.float32)).astype(jnp.bfloat16)


def multiply_kernel(plan, k, ahead, where_ref, fill_ref, table_ref, token_ref, inverse_ref, *refs):
    pieces, refs = refs[: plan.row_devices], refs[plan.row_devices + ahead :]
    keep_ref, send_ref, done_ref, upper_ref, lower_ref, rows_ref, both_ref, total_ref, sems = refs
    done_ref[0] = token_ref[0]
    row_index, col_index = where_ref[0], where_ref[1]
    core = col_index % 2
    count = table_ref[plan.count_row(k), 0]

    def fetch(number, slot):
        start = pl.multiple_of(table_ref[plan.block_row(k), number] * TILE, TILE)
        return pltpu.make_async_copy(inverse_ref.at[pl.ds(start, TILE), :], rows_ref.at[slot], sems.at[slot])

    for number in range(SLOTS - 1):

        @pl.when(number < count)
        def _(number=number):
            fetch(number, number).start()

    for shift in range(plan.row_devices):
        source = lax.rem(row_index - shift + plan.row_devices, plan.row_devices)
        for part in range(plan.per):
            start = pl.multiple_of(source * plan.own_rows + part * plan.high, plan.high)
            filled = fill_ref[k, (col_index * plan.block_rows + start) // TILE].astype(jnp.float32)
            high, low = split_high_low(pieces[shift][part * plan.high : (part + 1) * plan.high, :] * filled)
            upper_ref[pl.ds(start, plan.high), :] = high
            lower_ref[pl.ds(start, plan.high), :] = low

    def one(number, carry):
        slot = lax.rem(number, SLOTS)
        fetch(number, slot).wait()

        @pl.when(number + SLOTS - 1 < count)
        def _():
            fetch(number + SLOTS - 1, lax.rem(number + SLOTS - 1, SLOTS)).start()

        high, low = split_high_low(rows_ref[slot])
        both_ref[:TILE] = high
        both_ref[TILE:] = low
        first = jnp.dot(both_ref[...], upper_ref[...], preferred_element_type=jnp.float32)
        second = jnp.dot(both_ref[:TILE], lower_ref[...], preferred_element_type=jnp.float32)
        total_ref[...] = first[:TILE] + (first[TILE:] + second)
        for part in range(plan.sub):
            near = pl.multiple_of(part * plan.high + core * plan.half, plan.half)
            far = pl.multiple_of(part * plan.high + (1 - core) * plan.half, plan.half)
            keep_ref[number * plan.sub + part] = total_ref[pl.ds(near, plan.half), :]
            send_ref[number * plan.sub + part] = total_ref[pl.ds(far, plan.half), :]
        return carry

    lax.fori_loop(0, count, one, 0)


def multiply(plan, cap, k, where, fill_list, table, token, inverse, pieces, ahead):
    shape = jax.ShapeDtypeStruct((cap, plan.half, W), jnp.float32)
    smem, vmem, anywhere = (pl.BlockSpec(memory_space=space) for space in (SMEM, VMEM, pl.ANY))
    return pl.pallas_call(
        functools.partial(multiply_kernel, plan, k, len(ahead)),
        out_shape=(shape, shape, TOKEN),
        in_specs=[smem] * 4 + [anywhere] + [vmem] * len(pieces) + [anywhere] * len(ahead),
        out_specs=(vmem, vmem, smem),
        scratch_shapes=[
            VMEM((plan.block_rows, W), jnp.bfloat16),
            VMEM((plan.block_rows, W), jnp.bfloat16),
            VMEM((SLOTS, TILE, plan.block_rows), jnp.float32),
            VMEM((2 * TILE, plan.block_rows), jnp.bfloat16),
            VMEM((TILE, W), jnp.float32),
            pltpu.SemaphoreType.DMA((SLOTS,)),
        ],
        compiler_params=pltpu.CompilerParams(vmem_limit_bytes=MULTIPLY_VMEM),
        cost_estimate=LONG,
        name="multiply",
    )(where, fill_list, table, token, inverse, *pieces, *ahead)


def call_local(kernel, out_shape, tables, token, operands, name, scratch=(), ahead=()):
    vmem, smem = pl.BlockSpec(memory_space=VMEM), pl.BlockSpec(memory_space=SMEM)

    def body(*refs):
        tables_in, token_ref, rest = refs[: len(tables)], refs[len(tables)], refs[len(tables) + len(ahead) + 1 :]
        last = len(operands) + len(out_shape)
        rest[last][0] = token_ref[0]
        kernel(*tables_in, *rest[:last], *rest[last + 1 :])

    return pl.pallas_call(
        body,
        out_shape=tuple(jax.ShapeDtypeStruct(x.shape, x.dtype) for x in out_shape) + (TOKEN,),
        in_specs=[smem] * (len(tables) + 1) + [pl.BlockSpec(memory_space=pl.ANY)] * len(ahead) + [vmem] * len(operands),
        out_specs=(vmem,) * len(out_shape) + (smem,),
        scratch_shapes=scratch,
        compiler_params=pltpu.CompilerParams(vmem_limit_bytes=VMEM_LIMIT),
        cost_estimate=LONG,
        name=name,
    )(*tables, token, *ahead, *operands)


def tile_lists(plan, table_ref, k, step, order, outs):
    counts = plan.count_row(k)
    yield outs[0], plan.give_row(k, order, step), table_ref[counts, plan.give_count(order, step)]
    yield outs[1], plan.hold_row(k, order, step), table_ref[counts, plan.hold_count(order, step)]


def relay_kernel(in_ref, out_ref):
    out_ref[...] = in_ref[...]


def merge_kernel(plan, k, table_ref, keep_ref, core_ref, *outs):
    for number, (first, last, order) in enumerate(plan.strips[k]):
        for out_ref, row, count in tile_lists(plan, table_ref, k, 0, order, outs[2 * number : 2 * number + 2]):

            def one(slot, carry, out_ref=out_ref, row=row, first=first, last=last):
                tile = table_ref[row, slot]
                place = table_ref[plan.rank_row(k), tile // plan.sub] * plan.sub + tile % plan.sub
                out_ref[slot] = keep_ref[place, first:last, :] + core_ref[place, first:last, :]
                return carry

            lax.fori_loop(0, count, one, 0)


def step_kernel(plan, k, step, table_ref, *refs):
    strips = plan.strips[k]
    size = len(strips)
    for number, (_, _, order) in enumerate(strips):
        held_ref, came_ref = refs[number], refs[size + number]
        outs = refs[2 * size + 2 * number : 2 * size + 2 * number + 2]
        for out_ref, row, count in tile_lists(plan, table_ref, k, step, order, outs):

            def one(slot, carry, out_ref=out_ref, row=row, order=order, held_ref=held_ref, came_ref=came_ref):
                place = table_ref[plan.pos_row(k, order, step - 1), table_ref[row, slot]]
                out_ref[slot] = held_ref[place] + came_ref[place]
                return carry

            lax.fori_loop(0, count, one, 0)


def strip_shapes(cap, strip):
    return (jax.ShapeDtypeStruct((cap, strip[1] - strip[0], W), jnp.float32),) * 2


def collect_kernel(plan, k, where_ref, fill_ref, table_ref, *refs):
    strips = plan.strips[k]
    size = len(strips)
    held, came, (near_ref, far_ref) = refs[:size], refs[size : 2 * size], refs[2 * size :]
    row_index, col_index = where_ref[0], where_ref[1]
    for out_ref, owner in ((near_ref, col_index), (far_ref, col_index ^ 1)):
        for part in range(plan.per):
            tile = owner * plan.per + part
            active = fill_ref[k, (row_index * plan.tile_rows + tile) // plan.sub] != 0

            @pl.when(active)
            def _(out_ref=out_ref, tile=tile, part=part):
                for number, (first, last, order) in enumerate(strips):
                    source = table_ref[plan.pos_row(k, order, plan.steps - 1), tile]
                    out_ref[part, first:last, :] = -(held[number][source] + came[number][source])

            @pl.when(jnp.logical_not(active))
            def _(out_ref=out_ref, part=part):
                out_ref[part] = jnp.zeros(out_ref.shape[1:], jnp.float32)


def finish_kernel(plan, where_ref, factor_ref, *refs):
    parts, (block_ref, term_ref) = refs[: 2 * SIBS], refs[2 * SIBS :]
    core = where_ref[1] % 2
    for k in range(SIBS):
        near_ref, far_ref = parts[2 * k], parts[2 * k + 1]
        columns = slice(k * W, (k + 1) * W)
        for part in range(plan.per):
            near = pl.multiple_of(part * plan.high + core * plan.half, plan.half)
            far = pl.multiple_of(part * plan.high + (1 - core) * plan.half, plan.half)
            block_ref[pl.ds(near, plan.half), columns] = near_ref[part]
            block_ref[pl.ds(far, plan.half), columns] = far_ref[part]
        term_ref[columns, :] = lax.dot_general(
            factor_ref[:, columns],
            block_ref[:, columns],
            (((0,), (0,)), ((), ())),
            precision=lax.Precision.HIGHEST,
            preferred_element_type=jnp.float32,
        )


def toggled(value, mask, devices):
    return lax.ppermute(value, ("row", "col"), [(i, i ^ mask) for i in range(devices)])


def minus_sum_everywhere(plan, base, value):
    cols, devices = plan.col_devices, plan.row_devices * plan.col_devices
    me = lax.axis_index("row") * cols + lax.axis_index("col")
    masks = [1 << bit for bit in range(devices.bit_length() - 1)]
    row_masks = [m for m in masks if m >= cols]
    col_masks = [m for m in masks if m < cols]
    rest = col_masks[2:] + row_masks[1:]
    groups = [col_masks[:1], col_masks[1:2] + row_masks[:1]]
    groups += [rest[i : i + 2] for i in range(0, len(rest), 2)]

    def member(group):
        return sum(((me & mask) != 0).astype(jnp.int32) << n for n, mask in enumerate(group))

    def spread(group, number):
        return sum(mask for n, mask in enumerate(group) if number >> n & 1)

    for group in groups[:-1]:
        size = 1 << len(group)
        rows = value.shape[0] // size
        mine = member(group)
        sent = [
            toggled(lax.dynamic_slice_in_dim(value, (mine ^ d) * rows, rows, 0), spread(group, d), devices)
            for d in range(1, size)
        ]
        own = lax.dynamic_slice_in_dim(value, mine * rows, rows, 0)
        value = functools.reduce(jnp.add, sent, own)
        base = lax.dynamic_slice_in_dim(base, mine * rows, rows, 0)
    group = groups[-1]
    arrived = [toggled(value, spread(group, d), devices) for d in range(1, 1 << len(group))]
    mine = member(group)
    whole = jnp.stack([value] + arrived)
    ordered = [lax.dynamic_index_in_dim(whole, mine ^ n, 0, False) for n in range(1 << len(group))]
    value = base - functools.reduce(jnp.add, ordered)
    for group in reversed(groups[:-1]):
        size = 1 << len(group)
        mine = member(group)
        parts = [value] + [toggled(value, spread(group, d), devices) for d in range(1, size)]
        whole = jnp.stack(parts)
        value = jnp.concatenate([lax.dynamic_index_in_dim(whole, mine ^ n, 0, False) for n in range(size)])
    return value


def cross(plan, value):
    rows, cols = plan.row_devices, plan.col_devices
    if rows != 2:
        return value
    pairs = [(r * cols + c, (c & 1) * cols + (c & ~1 | r)) for r in range(rows) for c in range(cols)]
    return lax.ppermute(value, ("row", "col"), pairs)


def home(plan, value):
    rows, cols = plan.row_devices, plan.col_devices
    if rows != 2:
        pairs = [(rows * j + h, h * cols + j) for j in range(cols) for h in range(rows)]
    else:
        pairs = []
        for y in range(rows):
            for c in range(cols):
                pairs.append((y * cols + c, y * cols + ((c & 1) * cols + (c & ~1 | y)) // 2))
    return lax.ppermute(value, ("row", "col"), pairs)


def sparse(plan, caps, ancestor_inv, factor_rows, diagonal_inv, fill_list):
    rows, cols = plan.row_devices, plan.col_devices
    where = jnp.stack([lax.axis_index("row"), lax.axis_index("col")]).astype(jnp.int32)
    table = make_plan(plan, where, fill_list)
    pair = [(i, i ^ 1) for i in range(cols)]
    turns = [[(i, (i + shift) % rows) for i in range(rows)] for shift in range(1, rows)]
    tile_set = jax.ShapeDtypeStruct((plan.per, plan.half, W), jnp.float32)
    crossed = [cross(plan, factor_rows[:, k * W : (k + 1) * W]) for k in range(SIBS)]
    homes = [home(plan, value) for value in crossed]
    state = [None] * SIBS

    def exchange(k, number, made):
        held, came = [], []
        for n, strip in enumerate(plan.strips[k]):
            bit = 1 << plan.orders[strip[2]][number]
            came.append(lax.ppermute(made[2 * n], "col", [(i, i ^ bit) for i in range(cols)]))
            held.append(made[2 * n + 1])
        state[k] = held + came

    def product(k, token):
        pieces = [homes[k]] + [lax.ppermute(homes[k], "row", turn) for turn in turns]
        ahead = homes[1:2] + crossed[2:3] if k == 0 else []
        near, far, token = multiply(
            plan, caps[0], k, where, fill_list, table, token, ancestor_inv, pieces, ahead
        )
        state[k] = [near, lax.ppermute(far, "col", pair)]
        return token

    def merge(k, token):
        shapes = sum((strip_shapes(caps[1], strip) for strip in plan.strips[k]), ())
        *made, token = call_local(functools.partial(merge_kernel, plan, k), shapes, [table], token, state[k], "merge")
        exchange(k, 0, made)
        return token

    def step(k, number, token):
        shapes = sum((strip_shapes(caps[number + 1], strip) for strip in plan.strips[k]), ())
        kernel = functools.partial(step_kernel, plan, k, number)
        *made, token = call_local(kernel, shapes, [table], token, state[k], "step")
        exchange(k, number, made)
        return token

    def collect(k, token):
        kernel = functools.partial(collect_kernel, plan, k)
        tables = [where, fill_list, table]
        near, far, token = call_local(kernel, (tile_set, tile_set), tables, token, state[k], "collect")
        state[k] = [near, lax.ppermute(far, "col", pair)]
        return token

    token = jnp.zeros(TOKEN.shape, TOKEN.dtype)
    last = plan.steps - 1
    token = product(0, token)
    token = merge(0, token)
    homes[2], token = call_local(relay_kernel, (homes[2],), [], token, [homes[2]], "relay")
    token = product(1, token)
    token = step(0, 1, token)
    token = merge(1, token)
    token = product(2, token)
    token = step(0, 2, token)
    token = step(1, 1, token)
    token = merge(2, token)
    for number in range(3, plan.steps):
        token = step(0, number, token)
        token = step(1, number - 1, token)
        token = step(2, number - 2, token)
    token = collect(0, token)
    token = step(1, last, token)
    token = step(2, last - 1, token)
    token = collect(1, token)
    token = step(2, last, token)
    token = collect(2, token)
    shapes = (
        jax.ShapeDtypeStruct(factor_rows.shape, jnp.float32),
        jax.ShapeDtypeStruct((SIBS * W, W), jnp.float32),
    )
    kernel = functools.partial(finish_kernel, plan)
    column_block, term, _ = call_local(kernel, shapes, [where], token, [factor_rows] + sum(state, []), "finish")
    diagonal_block = minus_sum_everywhere(plan, diagonal_inv.reshape(term.shape), term)
    return column_block, diagonal_block.reshape(diagonal_inv.shape)


def row_masks(fill_list, first_row, row_count):
    positions = first_row + jnp.arange(row_count, dtype=jnp.int32)
    tile_index = positions // TILE
    one_hot = (
        tile_index[:, None] == jnp.arange(fill_list.shape[1], dtype=jnp.int32)[None, :]
    ).astype(jnp.float32)
    return jnp.dot(one_hot, fill_list.T.astype(jnp.float32), precision=lax.Precision.HIGHEST)


def dense(ancestor_inv, factor_rows, diagonal_inv, fill_list):
    row_devices, col_devices = lax.axis_size("row"), lax.axis_size("col")
    group_span = col_devices // row_devices
    own_rows = factor_rows.shape[0]
    band_rows, block_rows = ancestor_inv.shape
    row_index, col_index = lax.axis_index("row"), lax.axis_index("col")
    first_row = row_index * band_rows + col_index * own_rows
    wide_mask = jnp.repeat(row_masks(fill_list, first_row, own_rows), W, axis=1)
    masked = factor_rows * wide_mask
    band = lax.all_gather(masked, "col", axis=0, tiled=True)
    section = lax.dynamic_slice_in_dim(band, col_index % group_span * block_rows, block_rows, 0)
    section = jnp.where(row_index == col_index // group_span, section, jnp.zeros_like(section))
    product = jnp.dot(ancestor_inv, lax.psum(section, "row"), precision=lax.Precision.HIGHEST)
    summed = lax.psum_scatter(product, "col", scatter_dimension=0, tiled=True)
    column_block = -summed * wide_mask
    left_side = masked.reshape(own_rows, SIBS, W)
    right_side = column_block.reshape(own_rows, SIBS, W)
    local_term = jnp.einsum("rkw,rkv->kwv", left_side, right_side, precision=lax.Precision.HIGHEST)
    update = lax.psum(local_term, ("row", "col"))
    return column_block, diagonal_inv - update


def fill_groups(plan):
    devices = np.arange(plan.row_devices * plan.col_devices)
    found = {}
    for order in plan.orders:
        for step in range(plan.steps + 1):
            mask = sum(1 << bit for bit in order[:step])
            key = (devices // plan.col_devices) * plan.col_devices + (devices % plan.col_devices & mask)
            for value in np.unique(key):
                found[(key == value).tobytes()] = (key == value, step)
    member = np.stack([group for group, _ in found.values()], axis=1).astype(np.float32)
    return np.repeat(member, plan.per, axis=0), np.array([step for _, step in found.values()])


SHARES = (((22, 32), (12, 16), (7, 8), (4, 4), (2, 2)), ((26, 32), (14, 16), (8, 8), (4, 4), (2, 2)))


def local(ancestor_inv, factor_rows, diagonal_inv, fill_list):
    plan = Plan(
        lax.axis_size("row"), lax.axis_size("col"), factor_rows.shape[0], ancestor_inv.shape[0], ancestor_inv.shape[1]
    )
    member, levels = fill_groups(plan)
    block_of = np.arange(member.shape[0]) // plan.sub
    spread = np.zeros((fill_list.shape[1], member.shape[1]), np.float32)
    np.add.at(spread, block_of, member)
    found = jnp.dot(fill_list.astype(jnp.float32), spread, precision=lax.Precision.HIGHEST)
    limits, branches = [], []
    for shares in SHARES:
        caps = []
        for level in range(plan.steps + 1):
            size = plan.tile_rows >> level
            part, full = shares[min(level, len(shares) - 1)]
            caps.append(min(size, -(-size * part // full)))
        limits.append([caps[level] for level in levels])
        branches.append(functools.partial(sparse, plan, caps))
    branches.append(dense)
    over = jnp.any(found[None] > np.array(limits, np.float32)[:, None], axis=(1, 2))
    index = jnp.sum(over.astype(jnp.int32))
    return lax.switch(index, branches, ancestor_inv, factor_rows, diagonal_inv, fill_list)


def solution(mesh):
    placed = (P("row", "col"), P(("row", "col"), None), P(), P())
    return jax.shard_map(
        local, mesh=mesh, in_specs=placed, out_specs=(P(("row", "col"), None), P()), check_vma=False
    )
```

```python
import functools

import jax
import jax.numpy as jnp
import numpy as np
from jax import lax
from jax.experimental import pallas as pl
from jax.experimental.pallas import tpu as pltpu
from jax.sharding import PartitionSpec as P

W = 256
SIBS = 3
TILE = 256
VMEM_LIMIT = 32 * 1024 * 1024
MULTIPLY_VMEM = 32 * 1024 * 1024
STRIPS = (((0, 2, 0), (2, 4, 1)), ((0, 2, 0), (2, 4, 1)), ((0, 2, 0), (2, 4, 1)))
SLOTS = 6
TOKEN = jax.ShapeDtypeStruct((1,), jnp.int32)
LONG = pl.CostEstimate(flops=10**11, bytes_accessed=1, transcendentals=0)
SMEM = pltpu.SMEM
VMEM = pltpu.VMEM


class Plan:
    def __init__(self, row_devices, col_devices, own_rows, band_rows, block_rows):
        self.row_devices, self.col_devices = row_devices, col_devices
        self.own_rows, self.band_rows, self.block_rows = own_rows, band_rows, block_rows
        self.bits = col_devices.bit_length() - 1
        self.high = min(TILE, own_rows)
        self.half = self.high // 2
        self.sub = TILE // self.high
        self.per = own_rows // self.high
        self.tile_rows = band_rows // self.high
        self.blocks = band_rows // TILE
        first = list(range(1, self.bits))
        second = [2, 1] + first[2:] if self.bits > 2 else first
        self.steps = len(first)
        self.orders = (first, second)
        unit = self.half // 4
        self.strips = [[(a * unit, b * unit, order) for a, b, order in sibling] for sibling in STRIPS]
        every = [(order, step) for order in range(2) for step in range(self.steps)]
        self.sequences = list({self.sequence(*each): each for each in every}.values())

    @property
    def table_rows(self):
        return 3 + 6 * self.steps

    def block_row(self, k):
        return k * self.table_rows

    def rank_row(self, k):
        return k * self.table_rows + 1

    def count_row(self, k):
        return k * self.table_rows + 2

    def sequence(self, order, step):
        same = self.orders[0] == self.orders[1] or step > 2
        return (0 if same else order) * self.steps + step

    def pos_row(self, k, order, step):
        return k * self.table_rows + 3 + 3 * self.sequence(order, step)

    def give_row(self, k, order, step):
        return 1 + self.pos_row(k, order, step)

    def hold_row(self, k, order, step):
        return 2 + self.pos_row(k, order, step)

    def give_count(self, order, step):
        return 1 + 2 * self.sequence(order, step)

    def hold_count(self, order, step):
        return 1 + self.give_count(order, step)


def plan_kernel(plan, where_ref, fill_ref, table_ref):
    row_index, col_index = where_ref[0], where_ref[1]
    sequences = plan.sequences
    zero = jnp.int32(0)

    def one_sibling(k, carry):
        def one_block(block, count):
            table_ref[plan.block_row(k), count] = block
            table_ref[plan.rank_row(k), block] = count
            return count + fill_ref[k, row_index * plan.blocks + block]

        table_ref[plan.count_row(k), 0] = lax.fori_loop(0, plan.blocks, one_block, zero)

        def one_tile(tile, counts):
            apart = (tile // plan.per) ^ col_index

            def place(counts):
                result = []
                rank = table_ref[plan.rank_row(k), tile // plan.sub] * plan.sub + tile % plan.sub
                held_at = {plan.sequence(*each): counts[2 * n] for n, each in enumerate(sequences)}
                for number, (order, step) in enumerate(sequences):
                    held, sent = counts[2 * number], counts[2 * number + 1]
                    bits = plan.orders[order]
                    earlier = sum(1 << bit for bit in bits[:step])
                    here = 1 << bits[step]
                    table_ref[plan.pos_row(k, order, step), tile] = held
                    before = held_at[plan.sequence(order, step - 1)] if step else rank
                    table_ref[plan.hold_row(k, order, step), held] = before
                    table_ref[plan.give_row(k, order, step), sent] = before
                    keeps = (apart & (earlier | here)) == 0
                    gives = (apart & (earlier | here)) == here
                    result += [held + keeps.astype(jnp.int32), sent + gives.astype(jnp.int32)]
                return tuple(result)

            active = fill_ref[k, (row_index * plan.tile_rows + tile) // plan.sub] != 0
            return lax.cond(active, place, lambda counts: counts, counts)

        counts = lax.fori_loop(0, plan.tile_rows, one_tile, (zero,) * (2 * len(sequences)))
        for number, (order, step) in enumerate(sequences):
            table_ref[plan.count_row(k), plan.hold_count(order, step)] = counts[2 * number]
            table_ref[plan.count_row(k), plan.give_count(order, step)] = counts[2 * number + 1]
        return carry

    lax.fori_loop(0, SIBS, one_sibling, zero)


def make_plan(plan, where, fill_list):
    width = -(-max(plan.tile_rows + 1, 3 + 4 * plan.steps) // 128) * 128
    return pl.pallas_call(
        functools.partial(plan_kernel, plan),
        out_shape=jax.ShapeDtypeStruct((SIBS * plan.table_rows, width), jnp.int32),
        in_specs=[pl.BlockSpec(memory_space=SMEM)] * 2,
        out_specs=pl.BlockSpec(memory_space=SMEM),
        name="plan",
    )(where, fill_list)


def split_high_low(values):
    high = values.astype(jnp.bfloat16)
    return high, (values - high.astype(jnp.float32)).astype(jnp.bfloat16)


def multiply_kernel(plan, k, ahead, where_ref, fill_ref, table_ref, token_ref, inverse_ref, *refs):
    pieces, refs = refs[: plan.row_devices], refs[plan.row_devices + ahead :]
    keep_ref, send_ref, done_ref, upper_ref, lower_ref, rows_ref, both_ref, total_ref, sems = refs
    done_ref[0] = token_ref[0]
    row_index, col_index = where_ref[0], where_ref[1]
    core = col_index % 2
    count = table_ref[plan.count_row(k), 0]

    def fetch(number, slot):
        start = pl.multiple_of(table_ref[plan.block_row(k), number] * TILE, TILE)
        return pltpu.make_async_copy(inverse_ref.at[pl.ds(start, TILE), :], rows_ref.at[slot], sems.at[slot])

    for number in range(SLOTS - 1):

        @pl.when(number < count)
        def _(number=number):
            fetch(number, number).start()

    for shift in range(plan.row_devices):
        source = lax.rem(row_index - shift + plan.row_devices, plan.row_devices)
        for part in range(plan.per):
            start = pl.multiple_of(source * plan.own_rows + part * plan.high, plan.high)
            filled = fill_ref[k, (col_index * plan.block_rows + start) // TILE].astype(jnp.float32)
            high, low = split_high_low(pieces[shift][part * plan.high : (part + 1) * plan.high, :] * filled)
            upper_ref[pl.ds(start, plan.high), :] = high
            lower_ref[pl.ds(start, plan.high), :] = low

    def one(number, carry):
        slot = lax.rem(number, SLOTS)
        fetch(number, slot).wait()

        @pl.when(number + SLOTS - 1 < count)
        def _():
            fetch(number + SLOTS - 1, lax.rem(number + SLOTS - 1, SLOTS)).start()

        high, low = split_high_low(rows_ref[slot])
        both_ref[:TILE] = high
        both_ref[TILE:] = low
        first = jnp.dot(both_ref[...], upper_ref[...], preferred_element_type=jnp.float32)
        second = jnp.dot(both_ref[:TILE], lower_ref[...], preferred_element_type=jnp.float32)
        total_ref[...] = first[:TILE] + (first[TILE:] + second)
        for part in range(plan.sub):
            near = pl.multiple_of(part * plan.high + core * plan.half, plan.half)
            far = pl.multiple_of(part * plan.high + (1 - core) * plan.half, plan.half)
            keep_ref[number * plan.sub + part] = total_ref[pl.ds(near, plan.half), :]
            send_ref[number * plan.sub + part] = total_ref[pl.ds(far, plan.half), :]
        return carry

    lax.fori_loop(0, count, one, 0)


def multiply(plan, cap, k, where, fill_list, table, token, inverse, pieces, ahead):
    shape = jax.ShapeDtypeStruct((cap, plan.half, W), jnp.float32)
    smem, vmem, anywhere = (pl.BlockSpec(memory_space=space) for space in (SMEM, VMEM, pl.ANY))
    return pl.pallas_call(
        functools.partial(multiply_kernel, plan, k, len(ahead)),
        out_shape=(shape, shape, TOKEN),
        in_specs=[smem] * 4 + [anywhere] + [vmem] * len(pieces) + [anywhere] * len(ahead),
        out_specs=(vmem, vmem, smem),
        scratch_shapes=[
            VMEM((plan.block_rows, W), jnp.bfloat16),
            VMEM((plan.block_rows, W), jnp.bfloat16),
            VMEM((SLOTS, TILE, plan.block_rows), jnp.float32),
            VMEM((2 * TILE, plan.block_rows), jnp.bfloat16),
            VMEM((TILE, W), jnp.float32),
            pltpu.SemaphoreType.DMA((SLOTS,)),
        ],
        compiler_params=pltpu.CompilerParams(vmem_limit_bytes=MULTIPLY_VMEM),
        cost_estimate=LONG,
        name="multiply",
    )(where, fill_list, table, token, inverse, *pieces, *ahead)


def call_local(kernel, out_shape, tables, token, operands, name, scratch=(), ahead=()):
    vmem, smem = pl.BlockSpec(memory_space=VMEM), pl.BlockSpec(memory_space=SMEM)

    def body(*refs):
        tables_in, token_ref, rest = refs[: len(tables)], refs[len(tables)], refs[len(tables) + len(ahead) + 1 :]
        last = len(operands) + len(out_shape)
        rest[last][0] = token_ref[0]
        kernel(*tables_in, *rest[:last], *rest[last + 1 :])

    return pl.pallas_call(
        body,
        out_shape=tuple(jax.ShapeDtypeStruct(x.shape, x.dtype) for x in out_shape) + (TOKEN,),
        in_specs=[smem] * (len(tables) + 1) + [pl.BlockSpec(memory_space=pl.ANY)] * len(ahead) + [vmem] * len(operands),
        out_specs=(vmem,) * len(out_shape) + (smem,),
        scratch_shapes=scratch,
        compiler_params=pltpu.CompilerParams(vmem_limit_bytes=VMEM_LIMIT),
        cost_estimate=LONG,
        name=name,
    )(*tables, token, *ahead, *operands)


def tile_lists(plan, table_ref, k, step, order, outs):
    counts = plan.count_row(k)
    yield outs[0], plan.give_row(k, order, step), table_ref[counts, plan.give_count(order, step)]
    yield outs[1], plan.hold_row(k, order, step), table_ref[counts, plan.hold_count(order, step)]


def relay_kernel(in_ref, out_ref):
    out_ref[...] = in_ref[...]


def merge_kernel(plan, k, table_ref, keep_ref, core_ref, *outs):
    for number, (first, last, order) in enumerate(plan.strips[k]):
        for out_ref, row, count in tile_lists(plan, table_ref, k, 0, order, outs[2 * number : 2 * number + 2]):

            def one(slot, carry, out_ref=out_ref, row=row, first=first, last=last):
                place = table_ref[row, slot]
                out_ref[slot] = keep_ref[place, first:last, :] + core_ref[place, first:last, :]
                return carry

            lax.fori_loop(0, count, one, 0)


def step_kernel(plan, k, step, table_ref, *refs):
    strips = plan.strips[k]
    size = len(strips)
    for number, (_, _, order) in enumerate(strips):
        held_ref, came_ref = refs[number], refs[size + number]
        outs = refs[2 * size + 2 * number : 2 * size + 2 * number + 2]
        for out_ref, row, count in tile_lists(plan, table_ref, k, step, order, outs):

            def one(slot, carry, out_ref=out_ref, row=row, held_ref=held_ref, came_ref=came_ref):
                place = table_ref[row, slot]
                out_ref[slot] = held_ref[place] + came_ref[place]
                return carry

            lax.fori_loop(0, count, one, 0)


def strip_shapes(cap, strip):
    return (jax.ShapeDtypeStruct((cap, strip[1] - strip[0], W), jnp.float32),) * 2


def collect_kernel(plan, k, where_ref, fill_ref, table_ref, *refs):
    strips = plan.strips[k]
    size = len(strips)
    held, came, (near_ref, far_ref) = refs[:size], refs[size : 2 * size], refs[2 * size :]
    row_index, col_index = where_ref[0], where_ref[1]
    for out_ref, owner in ((near_ref, col_index), (far_ref, col_index ^ 1)):
        for part in range(plan.per):
            tile = owner * plan.per + part
            active = fill_ref[k, (row_index * plan.tile_rows + tile) // plan.sub] != 0

            @pl.when(active)
            def _(out_ref=out_ref, tile=tile, part=part):
                for number, (first, last, order) in enumerate(strips):
                    source = table_ref[plan.pos_row(k, order, plan.steps - 1), tile]
                    out_ref[part, first:last, :] = -(held[number][source] + came[number][source])

            @pl.when(jnp.logical_not(active))
            def _(out_ref=out_ref, part=part):
                out_ref[part] = jnp.zeros(out_ref.shape[1:], jnp.float32)


def put_rows(plan, where_ref, near_ref, far_ref, block_ref, columns):
    core = where_ref[1] % 2
    for part in range(plan.per):
        near = pl.multiple_of(part * plan.high + core * plan.half, plan.half)
        far = pl.multiple_of(part * plan.high + (1 - core) * plan.half, plan.half)
        block_ref[pl.ds(near, plan.half), columns] = near_ref[part]
        block_ref[pl.ds(far, plan.half), columns] = far_ref[part]


def term_of(factor_ref, block_ref, columns):
    return lax.dot_general(
        factor_ref[:, columns],
        block_ref[:, columns],
        (((0,), (0,)), ((), ())),
        precision=lax.Precision.HIGHEST,
        preferred_element_type=jnp.float32,
    )


def early_kernel(plan, where_ref, factor_ref, *refs):
    parts, (block_ref, term_ref) = refs[:-2], refs[-2:]
    for k in range(SIBS - 1):
        columns = slice(k * W, (k + 1) * W)
        put_rows(plan, where_ref, parts[2 * k], parts[2 * k + 1], block_ref, columns)
        term_ref[columns, :] = term_of(factor_ref, block_ref, columns)


def finish_kernel(plan, where_ref, factor_ref, early_ref, near_ref, far_ref, block_ref, term_ref):
    put_rows(plan, where_ref, near_ref, far_ref, block_ref, slice(0, W))
    term_ref[(SIBS - 1) * W :, :] = term_of(factor_ref, block_ref, slice(0, W))
    term_ref[: (SIBS - 1) * W, :] = early_ref[...]


def step_and_collect_kernel(plan, k, number, done, where_ref, fill_ref, table_ref, *refs):
    size, size_done = 2 * len(plan.strips[k]), 2 * len(plan.strips[done])
    inputs = size + size_done
    step_kernel(plan, k, number, table_ref, *refs[:size], *refs[inputs : inputs + size])
    collect_kernel(plan, done, where_ref, fill_ref, table_ref, *refs[size:inputs], *refs[inputs + size :])


def toggled(value, mask, devices):
    return lax.ppermute(value, ("row", "col"), [(i, i ^ mask) for i in range(devices)])


def minus_sum_everywhere(plan, base, value):
    cols, devices = plan.col_devices, plan.row_devices * plan.col_devices
    me = lax.axis_index("row") * cols + lax.axis_index("col")
    masks = [1 << bit for bit in range(devices.bit_length() - 1)]
    row_masks = [m for m in masks if m >= cols]
    col_masks = [m for m in masks if m < cols]
    rest = col_masks[2:] + row_masks[1:]
    groups = [col_masks[:1], col_masks[1:2] + row_masks[:1]]
    groups += [rest[i : i + 2] for i in range(0, len(rest), 2)]

    def member(group):
        return sum(((me & mask) != 0).astype(jnp.int32) << n for n, mask in enumerate(group))

    def spread(group, number):
        return sum(mask for n, mask in enumerate(group) if number >> n & 1)

    for group in groups[:-1]:
        size = 1 << len(group)
        rows = value.shape[0] // size
        mine = member(group)
        sent = [
            toggled(lax.dynamic_slice_in_dim(value, (mine ^ d) * rows, rows, 0), spread(group, d), devices)
            for d in range(1, size)
        ]
        own = lax.dynamic_slice_in_dim(value, mine * rows, rows, 0)
        value = functools.reduce(jnp.add, sent, own)
        base = lax.dynamic_slice_in_dim(base, mine * rows, rows, 0)
    group = groups[-1]
    arrived = [toggled(value, spread(group, d), devices) for d in range(1, 1 << len(group))]
    mine = member(group)
    whole = jnp.stack([value] + arrived)
    ordered = [lax.dynamic_index_in_dim(whole, mine ^ n, 0, False) for n in range(1 << len(group))]
    value = base - functools.reduce(jnp.add, ordered)
    for group in reversed(groups[:-1]):
        size = 1 << len(group)
        mine = member(group)
        parts = [value] + [toggled(value, spread(group, d), devices) for d in range(1, size)]
        whole = jnp.stack(parts)
        value = jnp.concatenate([lax.dynamic_index_in_dim(whole, mine ^ n, 0, False) for n in range(size)])
    return value


def cross(plan, value):
    rows, cols = plan.row_devices, plan.col_devices
    if rows != 2:
        return value
    pairs = [(r * cols + c, (c & 1) * cols + (c & ~1 | r)) for r in range(rows) for c in range(cols)]
    return lax.ppermute(value, ("row", "col"), pairs)


def home(plan, value):
    rows, cols = plan.row_devices, plan.col_devices
    if rows != 2:
        pairs = [(rows * j + h, h * cols + j) for j in range(cols) for h in range(rows)]
    else:
        pairs = []
        for y in range(rows):
            for c in range(cols):
                pairs.append((y * cols + c, y * cols + ((c & 1) * cols + (c & ~1 | y)) // 2))
    return lax.ppermute(value, ("row", "col"), pairs)


def sparse(plan, caps, ancestor_inv, factor_rows, diagonal_inv, fill_list):
    rows, cols = plan.row_devices, plan.col_devices
    where = jnp.stack([lax.axis_index("row"), lax.axis_index("col")]).astype(jnp.int32)
    table = make_plan(plan, where, fill_list)
    pair = [(i, i ^ 1) for i in range(cols)]
    turns = [[(i, (i + shift) % rows) for i in range(rows)] for shift in range(1, rows)]
    tile_set = jax.ShapeDtypeStruct((plan.per, plan.half, W), jnp.float32)
    crossed = [cross(plan, factor_rows[:, k * W : (k + 1) * W]) for k in range(SIBS)]
    homes = [home(plan, value) for value in crossed]
    state = [None] * SIBS

    def exchange(k, number, made):
        held, came = [], []
        for n, strip in enumerate(plan.strips[k]):
            bit = 1 << plan.orders[strip[2]][number]
            came.append(lax.ppermute(made[2 * n], "col", [(i, i ^ bit) for i in range(cols)]))
            held.append(made[2 * n + 1])
        state[k] = held + came

    def product(k, token):
        pieces = [homes[k]] + [lax.ppermute(homes[k], "row", turn) for turn in turns]
        ahead = homes[1:2] + crossed[2:3] if k == 0 else []
        near, far, token = multiply(
            plan, caps[0], k, where, fill_list, table, token, ancestor_inv, pieces, ahead
        )
        state[k] = [near, lax.ppermute(far, "col", pair)]
        return token

    def merge(k, token):
        shapes = sum((strip_shapes(caps[1], strip) for strip in plan.strips[k]), ())
        *made, token = call_local(functools.partial(merge_kernel, plan, k), shapes, [table], token, state[k], "merge")
        exchange(k, 0, made)
        return token

    def step(k, number, token):
        shapes = sum((strip_shapes(caps[number + 1], strip) for strip in plan.strips[k]), ())
        kernel = functools.partial(step_kernel, plan, k, number)
        *made, token = call_local(kernel, shapes, [table], token, state[k], "step")
        exchange(k, number, made)
        return token

    def collect(k, token):
        kernel = functools.partial(collect_kernel, plan, k)
        tables = [where, fill_list, table]
        near, far, token = call_local(kernel, (tile_set, tile_set), tables, token, state[k], "collect")
        state[k] = [near, lax.ppermute(far, "col", pair)]
        return token

    def step_and_collect(k, number, done, token):
        shapes = sum((strip_shapes(caps[number + 1], strip) for strip in plan.strips[k]), ())
        kernel = functools.partial(step_and_collect_kernel, plan, k, number, done)
        operands = state[k] + state[done]
        tables = [where, fill_list, table]
        *made, near, far, token = call_local(kernel, shapes + (tile_set,) * 2, tables, token, operands, "step_collect")
        state[done] = [near, lax.ppermute(far, "col", pair)]
        exchange(k, number, made)
        return token

    token = jnp.zeros(TOKEN.shape, TOKEN.dtype)
    last = plan.steps - 1
    token = product(0, token)
    token = merge(0, token)
    token = product(1, token)
    homes[2], token = call_local(relay_kernel, (homes[2],), [], token, [homes[2]], "relay")
    token = step(0, 1, token)
    token = merge(1, token)
    token = product(2, token)
    token = step(0, 2, token)
    token = step(1, 1, token)
    token = merge(2, token)
    for number in range(3, plan.steps):
        token = step(0, number, token)
        token = step(1, number - 1, token)
        token = step(2, number - 2, token)
    token = step_and_collect(1, last, 0, token)
    token = step(2, last - 1, token)
    token = collect(1, token)
    token = step(2, last, token)
    early_shapes = (
        jax.ShapeDtypeStruct((factor_rows.shape[0], (SIBS - 1) * W), jnp.float32),
        jax.ShapeDtypeStruct(((SIBS - 1) * W, W), jnp.float32),
    )
    operands = [factor_rows[:, : (SIBS - 1) * W]] + sum(state[:-1], [])
    early_block, early_term, token = call_local(
        functools.partial(early_kernel, plan), early_shapes, [where], token, operands, "early"
    )
    token = collect(2, token)
    shapes = (
        jax.ShapeDtypeStruct((factor_rows.shape[0], W), jnp.float32),
        jax.ShapeDtypeStruct((SIBS * W, W), jnp.float32),
    )
    operands = [factor_rows[:, (SIBS - 1) * W :], early_term] + state[-1]
    last_block, term, _ = call_local(functools.partial(finish_kernel, plan), shapes, [where], token, operands, "finish")
    column_block = jnp.concatenate([early_block, last_block], axis=1)
    diagonal_block = minus_sum_everywhere(plan, diagonal_inv.reshape(term.shape), term)
    return column_block, diagonal_block.reshape(diagonal_inv.shape)


def row_masks(fill_list, first_row, row_count):
    positions = first_row + jnp.arange(row_count, dtype=jnp.int32)
    tile_index = positions // TILE
    one_hot = (
        tile_index[:, None] == jnp.arange(fill_list.shape[1], dtype=jnp.int32)[None, :]
    ).astype(jnp.float32)
    return jnp.dot(one_hot, fill_list.T.astype(jnp.float32), precision=lax.Precision.HIGHEST)


def dense(ancestor_inv, factor_rows, diagonal_inv, fill_list):
    row_devices, col_devices = lax.axis_size("row"), lax.axis_size("col")
    group_span = col_devices // row_devices
    own_rows = factor_rows.shape[0]
    band_rows, block_rows = ancestor_inv.shape
    row_index, col_index = lax.axis_index("row"), lax.axis_index("col")
    first_row = row_index * band_rows + col_index * own_rows
    wide_mask = jnp.repeat(row_masks(fill_list, first_row, own_rows), W, axis=1)
    masked = factor_rows * wide_mask
    band = lax.all_gather(masked, "col", axis=0, tiled=True)
    section = lax.dynamic_slice_in_dim(band, col_index % group_span * block_rows, block_rows, 0)
    section = jnp.where(row_index == col_index // group_span, section, jnp.zeros_like(section))
    product = jnp.dot(ancestor_inv, lax.psum(section, "row"), precision=lax.Precision.HIGHEST)
    summed = lax.psum_scatter(product, "col", scatter_dimension=0, tiled=True)
    column_block = -summed * wide_mask
    left_side = masked.reshape(own_rows, SIBS, W)
    right_side = column_block.reshape(own_rows, SIBS, W)
    local_term = jnp.einsum("rkw,rkv->kwv", left_side, right_side, precision=lax.Precision.HIGHEST)
    update = lax.psum(local_term, ("row", "col"))
    return column_block, diagonal_inv - update


def fill_groups(plan):
    devices = np.arange(plan.row_devices * plan.col_devices)
    found = {}
    for order in plan.orders:
        for step in range(plan.steps + 1):
            mask = sum(1 << bit for bit in order[:step])
            key = (devices // plan.col_devices) * plan.col_devices + (devices % plan.col_devices & mask)
            for value in np.unique(key):
                found[(key == value).tobytes()] = (key == value, step)
    member = np.stack([group for group, _ in found.values()], axis=1).astype(np.float32)
    return np.repeat(member, plan.per, axis=0), np.array([step for _, step in found.values()])


SHARES = (
    ((22, 32), (11, 16), (7, 8), (4, 4), (2, 2)),
    ((22, 32), (12, 16), (7, 8), (4, 4), (2, 2)),
    ((26, 32), (14, 16), (8, 8), (4, 4), (2, 2)),
)


def local(ancestor_inv, factor_rows, diagonal_inv, fill_list):
    plan = Plan(
        lax.axis_size("row"), lax.axis_size("col"), factor_rows.shape[0], ancestor_inv.shape[0], ancestor_inv.shape[1]
    )
    member, levels = fill_groups(plan)
    block_of = np.arange(member.shape[0]) // plan.sub
    spread = np.zeros((fill_list.shape[1], member.shape[1]), np.float32)
    np.add.at(spread, block_of, member)
    found = jnp.dot(fill_list.astype(jnp.float32), spread, precision=lax.Precision.HIGHEST)
    limits, branches = [], []
    for shares in SHARES:
        caps = []
        for level in range(plan.steps + 1):
            size = plan.tile_rows >> level
            part, full = shares[min(level, len(shares) - 1)]
            caps.append(min(size, -(-size * part // full)))
        limits.append([caps[level] for level in levels])
        branches.append(functools.partial(sparse, plan, caps))
    branches.append(dense)
    over = jnp.any(found[None] > np.array(limits, np.float32)[:, None], axis=(1, 2))
    index = jnp.sum(over.astype(jnp.int32))
    return lax.switch(index, branches, ancestor_inv, factor_rows, diagonal_inv, fill_list)


def solution(mesh):
    placed = (P("row", "col"), P(("row", "col"), None), P(), P())
    return jax.shard_map(
        local, mesh=mesh, in_specs=placed, out_specs=(P(("row", "col"), None), P()), check_vma=False
    )
```

```python
import functools

import jax
import jax.numpy as jnp
import numpy as np
from jax import lax
from jax.experimental import pallas as pl
from jax.experimental.pallas import tpu as pltpu
from jax.sharding import PartitionSpec as P

W = 256
SIBS = 3
TILE = 256
VMEM_LIMIT = 32 * 1024 * 1024
MULTIPLY_VMEM = 32 * 1024 * 1024
STRIPS = (((0, 2, 0), (2, 4, 1)), ((0, 2, 0), (2, 4, 1)), ((0, 2, 0), (2, 4, 1)))
SLOTS = 8
TOKEN = jax.ShapeDtypeStruct((1,), jnp.int32)
LONG = pl.CostEstimate(flops=10**11, bytes_accessed=1, transcendentals=0)
SMEM = pltpu.SMEM
VMEM = pltpu.VMEM


class Plan:
    def __init__(self, row_devices, col_devices, own_rows, band_rows, block_rows):
        self.row_devices, self.col_devices = row_devices, col_devices
        self.own_rows, self.band_rows, self.block_rows = own_rows, band_rows, block_rows
        self.bits = col_devices.bit_length() - 1
        self.high = min(TILE, own_rows)
        self.half = self.high // 2
        self.sub = TILE // self.high
        self.per = own_rows // self.high
        self.tile_rows = band_rows // self.high
        self.blocks = band_rows // TILE
        first = list(range(1, self.bits))
        second = [2, 1] + first[2:] if self.bits > 2 else first
        self.steps = len(first)
        self.orders = (first, second)
        unit = self.half // 4
        self.strips = [[(a * unit, b * unit, order) for a, b, order in sibling] for sibling in STRIPS]
        every = [(order, step) for order in range(2) for step in range(self.steps)]
        self.sequences = list({self.sequence(*each): each for each in every}.values())

    @property
    def table_rows(self):
        return 3 + 6 * self.steps

    def block_row(self, k):
        return k * self.table_rows

    def rank_row(self, k):
        return k * self.table_rows + 1

    def count_row(self, k):
        return k * self.table_rows + 2

    def sequence(self, order, step):
        same = self.orders[0] == self.orders[1] or step > 2
        return (0 if same else order) * self.steps + step

    def pos_row(self, k, order, step):
        return k * self.table_rows + 3 + 3 * self.sequence(order, step)

    def give_row(self, k, order, step):
        return 1 + self.pos_row(k, order, step)

    def hold_row(self, k, order, step):
        return 2 + self.pos_row(k, order, step)

    def give_count(self, order, step):
        return 1 + 2 * self.sequence(order, step)

    def hold_count(self, order, step):
        return 1 + self.give_count(order, step)


def plan_kernel(plan, where_ref, fill_ref, table_ref):
    row_index, col_index = where_ref[0], where_ref[1]
    sequences = plan.sequences
    zero = jnp.int32(0)

    def one_sibling(k, carry):
        def one_block(block, count):
            table_ref[plan.block_row(k), count] = block
            table_ref[plan.rank_row(k), block] = count
            return count + fill_ref[k, row_index * plan.blocks + block]

        table_ref[plan.count_row(k), 0] = lax.fori_loop(0, plan.blocks, one_block, zero)

        def one_tile(tile, counts):
            apart = (tile // plan.per) ^ col_index

            def place(counts):
                result = []
                rank = table_ref[plan.rank_row(k), tile // plan.sub] * plan.sub + tile % plan.sub
                held_at = {plan.sequence(*each): counts[2 * n] for n, each in enumerate(sequences)}
                for number, (order, step) in enumerate(sequences):
                    held, sent = counts[2 * number], counts[2 * number + 1]
                    bits = plan.orders[order]
                    earlier = sum(1 << bit for bit in bits[:step])
                    here = 1 << bits[step]
                    if step == plan.steps - 1:
                        table_ref[plan.pos_row(k, order, step), tile] = held
                    before = held_at[plan.sequence(order, step - 1)] if step else rank
                    table_ref[plan.hold_row(k, order, step), held] = before
                    table_ref[plan.give_row(k, order, step), sent] = before
                    keeps = (apart & (earlier | here)) == 0
                    gives = (apart & (earlier | here)) == here
                    result += [held + keeps.astype(jnp.int32), sent + gives.astype(jnp.int32)]
                return tuple(result)

            active = fill_ref[k, (row_index * plan.tile_rows + tile) // plan.sub] != 0
            return lax.cond(active, place, lambda counts: counts, counts)

        counts = lax.fori_loop(0, plan.tile_rows, one_tile, (zero,) * (2 * len(sequences)))
        for number, (order, step) in enumerate(sequences):
            table_ref[plan.count_row(k), plan.hold_count(order, step)] = counts[2 * number]
            table_ref[plan.count_row(k), plan.give_count(order, step)] = counts[2 * number + 1]
        return carry

    lax.fori_loop(0, SIBS, one_sibling, zero)


def make_plan(plan, where, fill_list):
    width = -(-max(plan.tile_rows + 1, 3 + 4 * plan.steps) // 128) * 128
    return pl.pallas_call(
        functools.partial(plan_kernel, plan),
        out_shape=jax.ShapeDtypeStruct((SIBS * plan.table_rows, width), jnp.int32),
        in_specs=[pl.BlockSpec(memory_space=SMEM)] * 2,
        out_specs=pl.BlockSpec(memory_space=SMEM),
        name="plan",
    )(where, fill_list)


def split_high_low(values):
    high = values.astype(jnp.bfloat16)
    return high, (values - high.astype(jnp.float32)).astype(jnp.bfloat16)


def multiply_kernel(plan, k, ahead, where_ref, fill_ref, table_ref, token_ref, inverse_ref, *refs):
    pieces, refs = refs[: plan.row_devices], refs[plan.row_devices + ahead :]
    keep_ref, send_ref, done_ref, upper_ref, lower_ref, rows_ref, both_ref, total_ref, sems = refs
    done_ref[0] = token_ref[0]
    row_index, col_index = where_ref[0], where_ref[1]
    core = col_index % 2
    count = table_ref[plan.count_row(k), 0]

    def fetch(number, slot):
        start = pl.multiple_of(table_ref[plan.block_row(k), number] * TILE, TILE)
        return pltpu.make_async_copy(inverse_ref.at[pl.ds(start, TILE), :], rows_ref.at[slot], sems.at[slot])

    for number in range(SLOTS - 1):

        @pl.when(number < count)
        def _(number=number):
            fetch(number, number).start()

    for shift in range(plan.row_devices):
        source = lax.rem(row_index - shift + plan.row_devices, plan.row_devices)
        for part in range(plan.per):
            start = pl.multiple_of(source * plan.own_rows + part * plan.high, plan.high)
            filled = fill_ref[k, (col_index * plan.block_rows + start) // TILE].astype(jnp.float32)
            high, low = split_high_low(pieces[shift][part * plan.high : (part + 1) * plan.high, :] * filled)
            upper_ref[pl.ds(start, plan.high), :] = high
            lower_ref[pl.ds(start, plan.high), :] = low

    def one(number, carry):
        slot = lax.rem(number, SLOTS)
        fetch(number, slot).wait()

        @pl.when(number + SLOTS - 1 < count)
        def _():
            fetch(number + SLOTS - 1, lax.rem(number + SLOTS - 1, SLOTS)).start()

        high, low = split_high_low(rows_ref[slot])
        both_ref[:TILE] = high
        both_ref[TILE:] = low
        first = jnp.dot(both_ref[...], upper_ref[...], preferred_element_type=jnp.float32)
        second = jnp.dot(both_ref[:TILE], lower_ref[...], preferred_element_type=jnp.float32)
        total_ref[...] = first[:TILE] + (first[TILE:] + second)
        for part in range(plan.sub):
            near = pl.multiple_of(part * plan.high + core * plan.half, plan.half)
            far = pl.multiple_of(part * plan.high + (1 - core) * plan.half, plan.half)
            keep_ref[number * plan.sub + part] = total_ref[pl.ds(near, plan.half), :]
            send_ref[number * plan.sub + part] = total_ref[pl.ds(far, plan.half), :]
        return carry

    lax.fori_loop(0, count, one, 0)


def multiply(plan, cap, k, where, fill_list, table, token, inverse, pieces, ahead):
    shape = jax.ShapeDtypeStruct((cap, plan.half, W), jnp.float32)
    smem, vmem, anywhere = (pl.BlockSpec(memory_space=space) for space in (SMEM, VMEM, pl.ANY))
    return pl.pallas_call(
        functools.partial(multiply_kernel, plan, k, len(ahead)),
        out_shape=(shape, shape, TOKEN),
        in_specs=[smem] * 4 + [anywhere] + [vmem] * len(pieces) + [anywhere] * len(ahead),
        out_specs=(vmem, vmem, smem),
        scratch_shapes=[
            VMEM((plan.block_rows, W), jnp.bfloat16),
            VMEM((plan.block_rows, W), jnp.bfloat16),
            VMEM((SLOTS, TILE, plan.block_rows), jnp.float32),
            VMEM((2 * TILE, plan.block_rows), jnp.bfloat16),
            VMEM((TILE, W), jnp.float32),
            pltpu.SemaphoreType.DMA((SLOTS,)),
        ],
        compiler_params=pltpu.CompilerParams(vmem_limit_bytes=MULTIPLY_VMEM),
        cost_estimate=LONG,
        name="multiply",
    )(where, fill_list, table, token, inverse, *pieces, *ahead)


def call_local(kernel, out_shape, tables, token, operands, name, scratch=(), ahead=()):
    vmem, smem = pl.BlockSpec(memory_space=VMEM), pl.BlockSpec(memory_space=SMEM)

    def body(*refs):
        tables_in, token_ref, rest = refs[: len(tables)], refs[len(tables)], refs[len(tables) + len(ahead) + 1 :]
        last = len(operands) + len(out_shape)
        rest[last][0] = token_ref[0]
        kernel(*tables_in, *rest[:last], *rest[last + 1 :])

    return pl.pallas_call(
        body,
        out_shape=tuple(jax.ShapeDtypeStruct(x.shape, x.dtype) for x in out_shape) + (TOKEN,),
        in_specs=[smem] * (len(tables) + 1) + [pl.BlockSpec(memory_space=pl.ANY)] * len(ahead) + [vmem] * len(operands),
        out_specs=(vmem,) * len(out_shape) + (smem,),
        scratch_shapes=scratch,
        compiler_params=pltpu.CompilerParams(vmem_limit_bytes=VMEM_LIMIT),
        cost_estimate=LONG,
        name=name,
    )(*tables, token, *ahead, *operands)


def tile_lists(plan, table_ref, k, step, order, outs):
    counts = plan.count_row(k)
    yield outs[0], plan.give_row(k, order, step), table_ref[counts, plan.give_count(order, step)]
    yield outs[1], plan.hold_row(k, order, step), table_ref[counts, plan.hold_count(order, step)]


def relay_kernel(in_ref, out_ref):
    out_ref[...] = in_ref[...]


def merge_kernel(plan, k, table_ref, keep_ref, core_ref, *outs):
    for number, (first, last, order) in enumerate(plan.strips[k]):
        for out_ref, row, count in tile_lists(plan, table_ref, k, 0, order, outs[2 * number : 2 * number + 2]):

            def one(slot, carry, out_ref=out_ref, row=row, first=first, last=last):
                place = table_ref[row, slot]
                out_ref[slot] = keep_ref[place, first:last, :] + core_ref[place, first:last, :]
                return carry

            lax.fori_loop(0, count, one, 0)


def step_kernel(plan, k, step, table_ref, *refs):
    strips = plan.strips[k]
    size = len(strips)
    for number, (_, _, order) in enumerate(strips):
        held_ref, came_ref = refs[number], refs[size + number]
        outs = refs[2 * size + 2 * number : 2 * size + 2 * number + 2]
        for out_ref, row, count in tile_lists(plan, table_ref, k, step, order, outs):

            def one(slot, carry, out_ref=out_ref, row=row, held_ref=held_ref, came_ref=came_ref):
                place = table_ref[row, slot]
                out_ref[slot] = held_ref[place] + came_ref[place]
                return carry

            lax.fori_loop(0, count, one, 0)


def strip_shapes(cap, strip):
    return (jax.ShapeDtypeStruct((cap, strip[1] - strip[0], W), jnp.float32),) * 2


def collect_kernel(plan, k, where_ref, fill_ref, table_ref, *refs):
    strips = plan.strips[k]
    size = len(strips)
    held, came, (near_ref, far_ref) = refs[:size], refs[size : 2 * size], refs[2 * size :]
    row_index, col_index = where_ref[0], where_ref[1]
    for out_ref, owner in ((near_ref, col_index), (far_ref, col_index ^ 1)):
        for part in range(plan.per):
            tile = owner * plan.per + part
            active = fill_ref[k, (row_index * plan.tile_rows + tile) // plan.sub] != 0

            @pl.when(active)
            def _(out_ref=out_ref, tile=tile, part=part):
                for number, (first, last, order) in enumerate(strips):
                    source = table_ref[plan.pos_row(k, order, plan.steps - 1), tile]
                    out_ref[part, first:last, :] = -(held[number][source] + came[number][source])

            @pl.when(jnp.logical_not(active))
            def _(out_ref=out_ref, part=part):
                out_ref[part] = jnp.zeros(out_ref.shape[1:], jnp.float32)


def put_rows(plan, where_ref, near_ref, far_ref, block_ref, columns):
    core = where_ref[1] % 2
    for part in range(plan.per):
        near = pl.multiple_of(part * plan.high + core * plan.half, plan.half)
        far = pl.multiple_of(part * plan.high + (1 - core) * plan.half, plan.half)
        block_ref[pl.ds(near, plan.half), columns] = near_ref[part]
        block_ref[pl.ds(far, plan.half), columns] = far_ref[part]


def term_of(factor_ref, block_ref, columns):
    return lax.dot_general(
        factor_ref[:, columns],
        block_ref[:, columns],
        (((0,), (0,)), ((), ())),
        precision=lax.Precision.HIGHEST,
        preferred_element_type=jnp.float32,
    )


def early_kernel(plan, where_ref, factor_ref, *refs):
    parts, (block_ref, term_ref) = refs[:-2], refs[-2:]
    for k in range(SIBS - 1):
        columns = slice(k * W, (k + 1) * W)
        put_rows(plan, where_ref, parts[2 * k], parts[2 * k + 1], block_ref, columns)
        term_ref[columns, :] = term_of(factor_ref, block_ref, columns)


def finish_kernel(plan, where_ref, factor_ref, early_ref, near_ref, far_ref, block_ref, term_ref):
    put_rows(plan, where_ref, near_ref, far_ref, block_ref, slice(0, W))
    term_ref[(SIBS - 1) * W :, :] = term_of(factor_ref, block_ref, slice(0, W))
    term_ref[: (SIBS - 1) * W, :] = early_ref[...]


def step_and_collect_kernel(plan, k, number, done, where_ref, fill_ref, table_ref, *refs):
    size, size_done = 2 * len(plan.strips[k]), 2 * len(plan.strips[done])
    inputs = size + size_done
    step_kernel(plan, k, number, table_ref, *refs[:size], *refs[inputs : inputs + size])
    collect_kernel(plan, done, where_ref, fill_ref, table_ref, *refs[size:inputs], *refs[inputs + size :])


def toggled(value, mask, devices):
    return lax.ppermute(value, ("row", "col"), [(i, i ^ mask) for i in range(devices)])


def minus_sum_everywhere(plan, base, value):
    cols, devices = plan.col_devices, plan.row_devices * plan.col_devices
    me = lax.axis_index("row") * cols + lax.axis_index("col")
    masks = [1 << bit for bit in range(devices.bit_length() - 1)]
    row_masks = [m for m in masks if m >= cols]
    col_masks = [m for m in masks if m < cols]
    rest = col_masks[2:] + row_masks[1:]
    groups = [col_masks[:1], col_masks[1:2] + row_masks[:1]]
    groups += [rest[i : i + 2] for i in range(0, len(rest), 2)]

    def member(group):
        return sum(((me & mask) != 0).astype(jnp.int32) << n for n, mask in enumerate(group))

    def spread(group, number):
        return sum(mask for n, mask in enumerate(group) if number >> n & 1)

    for group in groups[:-1]:
        size = 1 << len(group)
        rows = value.shape[0] // size
        mine = member(group)
        sent = [
            toggled(lax.dynamic_slice_in_dim(value, (mine ^ d) * rows, rows, 0), spread(group, d), devices)
            for d in range(1, size)
        ]
        own = lax.dynamic_slice_in_dim(value, mine * rows, rows, 0)
        value = functools.reduce(jnp.add, sent, own)
        base = lax.dynamic_slice_in_dim(base, mine * rows, rows, 0)
    group = groups[-1]
    arrived = [toggled(value, spread(group, d), devices) for d in range(1, 1 << len(group))]
    mine = member(group)
    whole = jnp.stack([value] + arrived)
    ordered = [lax.dynamic_index_in_dim(whole, mine ^ n, 0, False) for n in range(1 << len(group))]
    value = base - functools.reduce(jnp.add, ordered)
    for group in reversed(groups[:-1]):
        size = 1 << len(group)
        mine = member(group)
        parts = [value] + [toggled(value, spread(group, d), devices) for d in range(1, size)]
        whole = jnp.stack(parts)
        value = jnp.concatenate([lax.dynamic_index_in_dim(whole, mine ^ n, 0, False) for n in range(size)])
    return value


def cross(plan, value):
    rows, cols = plan.row_devices, plan.col_devices
    if rows != 2:
        return value
    pairs = [(r * cols + c, (c & 1) * cols + (c & ~1 | r)) for r in range(rows) for c in range(cols)]
    return lax.ppermute(value, ("row", "col"), pairs)


def home(plan, value):
    rows, cols = plan.row_devices, plan.col_devices
    if rows != 2:
        pairs = [(rows * j + h, h * cols + j) for j in range(cols) for h in range(rows)]
    else:
        pairs = []
        for y in range(rows):
            for c in range(cols):
                pairs.append((y * cols + c, y * cols + ((c & 1) * cols + (c & ~1 | y)) // 2))
    return lax.ppermute(value, ("row", "col"), pairs)


def sparse(plan, caps, ancestor_inv, factor_rows, diagonal_inv, fill_list):
    rows, cols = plan.row_devices, plan.col_devices
    where = jnp.stack([lax.axis_index("row"), lax.axis_index("col")]).astype(jnp.int32)
    table = make_plan(plan, where, fill_list)
    pair = [(i, i ^ 1) for i in range(cols)]
    turns = [[(i, (i + shift) % rows) for i in range(rows)] for shift in range(1, rows)]
    tile_set = jax.ShapeDtypeStruct((plan.per, plan.half, W), jnp.float32)
    crossed = [cross(plan, factor_rows[:, k * W : (k + 1) * W]) for k in range(SIBS)]
    homes = [home(plan, value) for value in crossed]
    state = [None] * SIBS

    def exchange(k, number, made):
        held, came = [], []
        for n, strip in enumerate(plan.strips[k]):
            bit = 1 << plan.orders[strip[2]][number]
            came.append(lax.ppermute(made[2 * n], "col", [(i, i ^ bit) for i in range(cols)]))
            held.append(made[2 * n + 1])
        state[k] = held + came

    def product(k, token):
        pieces = [homes[k]] + [lax.ppermute(homes[k], "row", turn) for turn in turns]
        ahead = homes[1:2] + crossed[2:3] if k == 0 else []
        near, far, token = multiply(
            plan, caps[0], k, where, fill_list, table, token, ancestor_inv, pieces, ahead
        )
        state[k] = [near, lax.ppermute(far, "col", pair)]
        return token

    def merge(k, token):
        shapes = sum((strip_shapes(caps[1], strip) for strip in plan.strips[k]), ())
        *made, token = call_local(functools.partial(merge_kernel, plan, k), shapes, [table], token, state[k], "merge")
        exchange(k, 0, made)
        return token

    def step(k, number, token):
        shapes = sum((strip_shapes(caps[number + 1], strip) for strip in plan.strips[k]), ())
        kernel = functools.partial(step_kernel, plan, k, number)
        *made, token = call_local(kernel, shapes, [table], token, state[k], "step")
        exchange(k, number, made)
        return token

    def collect(k, token):
        kernel = functools.partial(collect_kernel, plan, k)
        tables = [where, fill_list, table]
        near, far, token = call_local(kernel, (tile_set, tile_set), tables, token, state[k], "collect")
        state[k] = [near, lax.ppermute(far, "col", pair)]
        return token

    def step_and_collect(k, number, done, token):
        shapes = sum((strip_shapes(caps[number + 1], strip) for strip in plan.strips[k]), ())
        kernel = functools.partial(step_and_collect_kernel, plan, k, number, done)
        operands = state[k] + state[done]
        tables = [where, fill_list, table]
        *made, near, far, token = call_local(kernel, shapes + (tile_set,) * 2, tables, token, operands, "step_collect")
        state[done] = [near, lax.ppermute(far, "col", pair)]
        exchange(k, number, made)
        return token

    token = jnp.zeros(TOKEN.shape, TOKEN.dtype)
    last = plan.steps - 1
    token = product(0, token)
    token = merge(0, token)
    token = product(1, token)
    homes[2], token = call_local(relay_kernel, (homes[2],), [], token, [homes[2]], "relay")
    token = step(0, 1, token)
    token = merge(1, token)
    token = product(2, token)
    token = step(0, 2, token)
    token = step(1, 1, token)
    token = merge(2, token)
    for number in range(3, plan.steps):
        token = step(0, number, token)
        token = step(1, number - 1, token)
        token = step(2, number - 2, token)
    token = step_and_collect(1, last, 0, token)
    token = step(2, last - 1, token)
    token = collect(1, token)
    token = step(2, last, token)
    early_shapes = (
        jax.ShapeDtypeStruct((factor_rows.shape[0], (SIBS - 1) * W), jnp.float32),
        jax.ShapeDtypeStruct(((SIBS - 1) * W, W), jnp.float32),
    )
    operands = [factor_rows[:, : (SIBS - 1) * W]] + sum(state[:-1], [])
    early_block, early_term, token = call_local(
        functools.partial(early_kernel, plan), early_shapes, [where], token, operands, "early"
    )
    token = collect(2, token)
    shapes = (
        jax.ShapeDtypeStruct((factor_rows.shape[0], W), jnp.float32),
        jax.ShapeDtypeStruct((SIBS * W, W), jnp.float32),
    )
    operands = [factor_rows[:, (SIBS - 1) * W :], early_term] + state[-1]
    last_block, term, _ = call_local(functools.partial(finish_kernel, plan), shapes, [where], token, operands, "finish")
    column_block = jnp.concatenate([early_block, last_block], axis=1)
    diagonal_block = minus_sum_everywhere(plan, diagonal_inv.reshape(term.shape), term)
    return column_block, diagonal_block.reshape(diagonal_inv.shape)


def row_masks(fill_list, first_row, row_count):
    positions = first_row + jnp.arange(row_count, dtype=jnp.int32)
    tile_index = positions // TILE
    one_hot = (
        tile_index[:, None] == jnp.arange(fill_list.shape[1], dtype=jnp.int32)[None, :]
    ).astype(jnp.float32)
    return jnp.dot(one_hot, fill_list.T.astype(jnp.float32), precision=lax.Precision.HIGHEST)


def dense(ancestor_inv, factor_rows, diagonal_inv, fill_list):
    row_devices, col_devices = lax.axis_size("row"), lax.axis_size("col")
    group_span = col_devices // row_devices
    own_rows = factor_rows.shape[0]
    band_rows, block_rows = ancestor_inv.shape
    row_index, col_index = lax.axis_index("row"), lax.axis_index("col")
    first_row = row_index * band_rows + col_index * own_rows
    wide_mask = jnp.repeat(row_masks(fill_list, first_row, own_rows), W, axis=1)
    masked = factor_rows * wide_mask
    band = lax.all_gather(masked, "col", axis=0, tiled=True)
    section = lax.dynamic_slice_in_dim(band, col_index % group_span * block_rows, block_rows, 0)
    section = jnp.where(row_index == col_index // group_span, section, jnp.zeros_like(section))
    product = jnp.dot(ancestor_inv, lax.psum(section, "row"), precision=lax.Precision.HIGHEST)
    summed = lax.psum_scatter(product, "col", scatter_dimension=0, tiled=True)
    column_block = -summed * wide_mask
    left_side = masked.reshape(own_rows, SIBS, W)
    right_side = column_block.reshape(own_rows, SIBS, W)
    local_term = jnp.einsum("rkw,rkv->kwv", left_side, right_side, precision=lax.Precision.HIGHEST)
    update = lax.psum(local_term, ("row", "col"))
    return column_block, diagonal_inv - update


def fill_groups(plan):
    devices = np.arange(plan.row_devices * plan.col_devices)
    found = {}
    for order in plan.orders:
        for step in range(plan.steps + 1):
            mask = sum(1 << bit for bit in order[:step])
            key = (devices // plan.col_devices) * plan.col_devices + (devices % plan.col_devices & mask)
            for value in np.unique(key):
                found[(key == value).tobytes()] = (key == value, step)
    member = np.stack([group for group, _ in found.values()], axis=1).astype(np.float32)
    return np.repeat(member, plan.per, axis=0), np.array([step for _, step in found.values()])


SHARES = (((22, 32), (12, 16), (7, 8), (4, 4), (2, 2)), ((26, 32), (14, 16), (8, 8), (4, 4), (2, 2)))


def local(ancestor_inv, factor_rows, diagonal_inv, fill_list):
    plan = Plan(
        lax.axis_size("row"), lax.axis_size("col"), factor_rows.shape[0], ancestor_inv.shape[0], ancestor_inv.shape[1]
    )
    member, levels = fill_groups(plan)
    block_of = np.arange(member.shape[0]) // plan.sub
    spread = np.zeros((fill_list.shape[1], member.shape[1]), np.float32)
    np.add.at(spread, block_of, member)
    found = jnp.dot(fill_list.astype(jnp.float32), spread, precision=lax.Precision.HIGHEST)
    limits, branches = [], []
    for shares in SHARES:
        caps = []
        for level in range(plan.steps + 1):
            size = plan.tile_rows >> level
            part, full = shares[min(level, len(shares) - 1)]
            caps.append(min(size, -(-size * part // full)))
        limits.append([caps[level] for level in levels])
        branches.append(functools.partial(sparse, plan, caps))
    branches.append(dense)
    over = jnp.any(found[None] > np.array(limits, np.float32)[:, None], axis=(1, 2))
    index = jnp.sum(over.astype(jnp.int32))
    return lax.switch(index, branches, ancestor_inv, factor_rows, diagonal_inv, fill_list)


def solution(mesh):
    placed = (P("row", "col"), P(("row", "col"), None), P(), P())
    return jax.shard_map(
        local, mesh=mesh, in_specs=placed, out_specs=(P(("row", "col"), None), P()), check_vma=False
    )
```
